32 devices in a mesh: groups: 2 (over x), dp: 16 (over z, y, core).
Axes of the slice: x: 2, y: 2, z: 4, core: 2. Of those that a mesh axis runs over, the one named last changes fastest.
Arguments:
- tokens: bfloat16 [32, 320, 1280], P(('groups', 'dp')), parts along dimension 0, may hold values from -6 to 6
- route: int32 [32, 320, 1], P(('groups', 'dp')), parts along dimension 0, may hold values from 0 to 3; in each aligned block of 320 rows (0 to 319, 320 to 639, ..., all dimensions but the last counted through in order) at most 124 rows name the same one
- labels: int32 [32], P(('groups', 'dp')), parts along dimension 0, may hold values from 0 to 15, each once
- moe_gain: float32 [1280], replicated, may hold values from 0.1 to 1.9
- router: bfloat16 [1280, 4], replicated, may hold values from -0.15625 to 0.15625
- w_in: bfloat16 [16, 1280, 1280], P('dp'), may hold values from -0.15625 to 0.15625
- w_out: bfloat16 [16, 1280, 1280], P('dp'), may hold values from -0.078125 to 0.078125
- out_gain: float32 [1280], replicated, may hold values from 0.1 to 1.9
- pool_query: float32 [2, 16, 80], replicated
- proj: bfloat16 [1280, 1280], replicated, may hold values from -0.15625 to 0.15625
- logit_scale: float32 [1], replicated
Outputs:
- mixed: bfloat16 [32, 320, 1280], P(('groups', 'dp')), parts along dimension 0
- d_pooled: float32 [32, 2, 1280], P(('groups', 'dp')), parts along dimension 0
- grad_proj: float32 [2560, 1280], P('groups'), parts along dimension 0
- loss: float32 [2], P('groups'), parts along dimension 0
The draws below stay inside these ranges and needn't reach their ends.
There are 2 independent parts, one for each index of `groups`. The reference program is written for one: setup_inputs(seed, part) draws one part's arguments, and reference() takes and returns one part's arrays. A program takes and returns all parts, laid end to end along the dimension named above; an argument that names none is the same for every part. Nothing has to cross between parts.
Inputs may be any that keep to these rules, and one draw needn't show every extreme that they name: `route`: within the rows of one device no expert is named more than 124 times, and in some device one expert is named exactly 124 times. `labels`: A permutation of the pairs.
All inputs are finite; a program needn't handle non-finite values.
Results may differ from the reference program's by a relative error of at most 0.017.
The reference program's roundings to bfloat16 on the way (of `normed`, `hidden`, `part` and `pooled`) count: a program that leaves them out, or rounds other values in their place, can miss the bound.
Values may be sent and summed in bfloat16 or wider, within the bound.
No kernel may reach another device: no remote copies, remote signals or barrier semaphores. Data moves between devices by JAX's collectives and lax.ppermute only.
A program may use at most 128 MiB of HBM per device.

```python
import math
import jax
import jax.numpy as jnp
import numpy as np
from jax import lax

D = 1280
FF = 5120
HEADS = 16
IMG_TOK = 256
SPLIT = 4
HEAD_DIM = 80
SEQ = 320
TOK_DEV = 320
PAIRS = 16
EXPERTS = 4
FF_DEV = 1280
CAP = 124
N_DP = 16


def draw_pool_query(key, part):
    key = jax.random.fold_in(key, 11)
    base = 2.0 * jax.random.normal(key, (2, HEADS, HEAD_DIM), jnp.float32)
    return base


def draw_logit_scale(key, part):
    key = jax.random.fold_in(key, 12)
    return jax.random.uniform(key, (1,), jnp.float32, 10.0, 30.0)


def levels(key, extent, pieces, low, top_value):
    def one(axis_at, parts):
        heights = jax.random.uniform(jax.random.fold_in(jax.random.fold_in(key, 6), axis_at), (parts,), jnp.float32, low / len(pieces), top_value / len(pieces))
        return jnp.repeat(jnp.exp(heights), extent[axis_at] // parts).reshape((-1,) + (1,) * (len(extent) - axis_at - 1))

    level = one(*pieces[0])
    for cut in pieces[1:]:
        level = level * one(*cut)
    return level


def shared_out(key, own, number, rows, number_of, top, most, lean):
    order = jax.random.permutation(key, number_of)
    heavy_load, ordinary = portions_of(number_of, rows * top, most, lean, True), portions_of(number_of, rows * top, most, lean, False)
    places = jnp.arange(number_of)

    def named(lengths, rotation):
        used = int((lengths > 0).sum())
        fixed = max(1, used // 4)
        passed = fixed + (places - fixed + rotation * (used - fixed)) % max(1, number_of - fixed)
        return jnp.zeros((number_of,), jnp.int32).at[order[jnp.where(places < fixed, places, passed)]].set(jnp.asarray(lengths, jnp.int32))

    lengths = jnp.where(number % 4 == 0, named(heavy_load, number // 4), named(ordinary, number - number // 4 - 1))
    mixed = jax.random.permutation(jax.random.fold_in(own, 3), number_of)
    giver, receiver = mixed[0:number_of // 2 * 2:2], mixed[1:number_of // 2 * 2:2]
    margin = jnp.minimum(lengths[giver] - 1, most - lengths[receiver]) // 2
    margin = jnp.where((giver == order[0]) | (receiver == order[0]) | (lengths[receiver] == 0), 0, jnp.maximum(margin, 0))
    passed = jax.random.randint(jax.random.fold_in(own, 4), (number_of // 2,), 0, 1 << 20) % (margin + 1)
    lengths = lengths.at[giver].add(-passed).at[receiver].add(passed)
    members = jnp.searchsorted(jnp.cumsum(lengths), jnp.arange(rows * top), side="right").astype(jnp.int32)
    grid = members.reshape(top, rows).T
    grid = grid[jax.random.permutation(jax.random.fold_in(own, 1), rows)]
    rotation = jax.random.randint(jax.random.fold_in(own, 2), (rows, 1), 0, top)
    return jnp.take_along_axis(grid, (jnp.arange(top)[None, :] + rotation) % top, axis=1)


def portions_of(number_of, total, reach, lean, full):
    weights = [(1 << 20) // math.isqrt(standing ** lean) + 1 for standing in range(1, number_of + 1)]
    largest = reach if full else min(reach, max(-(-total // number_of), total * weights[0] // sum(weights)))
    least = 1 if total - largest >= number_of - 1 else 0
    holding, surplus = [largest] + [least] * (number_of - 1), total - largest - least * (number_of - 1)
    while surplus > 0:
        candidates = [i for i in range(1, number_of) if holding[i] < largest] or [i for i in range(1, number_of) if holding[i] < reach]
        mass, budget = sum([weights[i] for i in candidates]), surplus
        for i in candidates:
            more = min(reach - holding[i], max(1, budget * weights[i] // mass), surplus)
            holding[i] = holding[i] + more
            surplus = surplus - more
    return np.array(holding)


def centred(key, extent, width, bound, shards=(), kind=jnp.bfloat16):
    level = levels(key, extent, shards, -0.22, 0.18) if shards else 1.0
    values = jax.random.normal(key, extent, jnp.float32) * width * level
    return jnp.minimum(jnp.maximum(values, -bound), bound).astype(kind)


def setup_inputs(seed: int = 0, part: int = 0) -> dict:
    streams_of = jax.random.split(jax.random.key(seed), 12)
    part_keys = jax.random.split(jax.random.fold_in(streams_of[11], part), 12)
    tokens = centred(part_keys[0], (PAIRS, SEQ, D), 1.0, 6.0, ((0, 16),))
    route_keys = jax.random.split(jax.random.fold_in(part_keys[1], 1), PAIRS * SEQ // TOK_DEV)
    route_turns = jax.random.permutation(jax.random.fold_in(part_keys[1], 3), PAIRS * SEQ // TOK_DEV)
    route = jax.vmap(lambda own, number: shared_out(jax.random.fold_in(part_keys[1], 2), own, number, TOK_DEV, EXPERTS, 1, CAP, 2))(route_keys, route_turns).reshape((PAIRS, SEQ, 1))
    labels = jax.random.permutation(part_keys[2], PAIRS).astype(jnp.int32)
    moe_gain = jnp.clip(1.0 + 0.18 * jax.random.normal(streams_of[3], (D,), jnp.float32), 0.1, 1.9)
    router = centred(streams_of[4], (D, EXPERTS), D ** -0.5, 0.15625)
    w_in = centred(streams_of[5], (N_DP, D, FF_DEV), D ** -0.5, 0.15625, ((0, 16),))
    w_out = centred(streams_of[6], (N_DP, FF_DEV, D), FF ** -0.5, 0.078125, ((0, 16),))
    out_gain = jnp.clip(1.0 + 0.18 * jax.random.normal(streams_of[7], (D,), jnp.float32), 0.1, 1.9)
    pool_query = draw_pool_query(jax.random.fold_in(streams_of[11], 71), part)
    proj = centred(streams_of[9], (D, D), D ** -0.5, 0.15625)
    logit_scale = draw_logit_scale(jax.random.fold_in(streams_of[11], 71), part)
    return dict(tokens=tokens, route=route, labels=labels, moe_gain=moe_gain, router=router, w_in=w_in, w_out=w_out, out_gain=out_gain, pool_query=pool_query, proj=proj, logit_scale=logit_scale)


def layer_norm(values, gain):
    mean = lax.optimization_barrier(jnp.mean(values, axis=-1, keepdims=True))
    centered = values - mean
    var = lax.optimization_barrier(jnp.mean(centered * centered, axis=-1, keepdims=True))
    return centered * lax.rsqrt(var + 1e-06) * gain

def pool(mixed, out_gain, pool_query):
    z_all = layer_norm(mixed.astype(jnp.float32), out_gain)
    count = z_all.shape[0]
    z_all = z_all.reshape(count, SEQ, HEADS, HEAD_DIM)
    result = []
    for modal, (lower, upper) in enumerate(((0, IMG_TOK), (IMG_TOK, SEQ))):
        piece = z_all[:, lower:upper]
        scores = jnp.einsum('pthd,hd->pht', piece, pool_query[modal], precision=lax.Precision.HIGHEST) / math.sqrt(HEAD_DIM)
        scores = scores - lax.optimization_barrier(jnp.max(scores, axis=-1, keepdims=True))
        weights = jnp.exp(scores)
        weights = weights / lax.optimization_barrier(jnp.sum(weights, axis=-1, keepdims=True))
        summed = jnp.einsum('pht,pthd->phd', weights, piece, precision=lax.Precision.HIGHEST)
        result.append(summed.reshape(count, D))
    return jnp.stack(result, axis=1).astype(jnp.bfloat16)

def contrast(emb, labels, logit_scale):
    count = emb.shape[0]
    norm = jnp.sqrt(lax.optimization_barrier(jnp.sum(emb * emb, axis=-1)) + 1e-06)
    unit = emb / norm[..., None]
    logits = logit_scale[0] * jnp.dot(unit[:, 0], unit[:, 1].T, precision=lax.Precision.HIGHEST)
    target = (labels[:, None] == jnp.arange(count, dtype=jnp.int32)[None, :]).astype(jnp.float32)
    row_top = lax.optimization_barrier(jnp.max(logits, axis=1, keepdims=True))
    row_exp = jnp.exp(logits - row_top)
    row_total = lax.optimization_barrier(jnp.sum(row_exp, axis=1, keepdims=True))
    row_lse = jnp.log(row_total) + row_top
    col_top = lax.optimization_barrier(jnp.max(logits, axis=0, keepdims=True))
    col_exp = jnp.exp(logits - col_top)
    col_total = lax.optimization_barrier(jnp.sum(col_exp, axis=0, keepdims=True))
    col_lse = jnp.log(col_total) + col_top
    matched = jnp.sum(logits * target)
    loss = (jnp.sum(row_lse) + jnp.sum(col_lse) - 2.0 * matched) / (2.0 * count)
    grad = logit_scale[0] * (row_exp / row_total + col_exp / col_total - 2.0 * target) / (2.0 * count)
    d_image = jnp.dot(grad, unit[:, 1], precision=lax.Precision.HIGHEST)
    d_text = jnp.dot(grad.T, unit[:, 0], precision=lax.Precision.HIGHEST)
    d_unit = jnp.stack([d_image, d_text], axis=1)
    d_emb = (d_unit - unit * lax.optimization_barrier(jnp.sum(unit * d_unit, axis=-1, keepdims=True))) / norm[..., None]
    return (loss.reshape(1), d_emb)

def reference(tokens, route, labels, moe_gain, router, w_in, w_out, out_gain, pool_query, proj, logit_scale):
    normed = layer_norm(tokens.astype(jnp.float32), moe_gain).astype(jnp.bfloat16)
    flat = normed.reshape(N_DP, TOK_DEV, D)
    ids = route.reshape(N_DP, TOK_DEV)
    onehot = (ids[..., None] == jnp.arange(EXPERTS, dtype=jnp.int32)).astype(jnp.int32)
    slot = lax.optimization_barrier(jnp.sum((jnp.cumsum(onehot, axis=1) - 1) * onehot, axis=2))
    place = ids * CAP + slot
    flat_place = (jnp.arange(N_DP, dtype=jnp.int32)[:, None] * (EXPERTS * CAP) + place).reshape(-1).astype(jnp.int32)
    buffer = jnp.zeros((N_DP * EXPERTS * CAP, D), jnp.bfloat16).at[flat_place].set(flat.reshape(-1, D))
    per_expert = buffer.reshape(N_DP, EXPERTS, CAP, D).transpose(1, 0, 2, 3).reshape(EXPERTS, N_DP * CAP, D)
    w_in_e = w_in.reshape(EXPERTS, SPLIT, D, FF_DEV)
    w_out_e = w_out.reshape(EXPERTS, SPLIT, FF_DEV, D)

    def run(items):
        rows, first, second = items
        total = jnp.zeros((rows.shape[0], D), jnp.float32)
        for quarter in range(SPLIT):
            hidden = jax.nn.gelu(jnp.dot(rows, first[quarter], preferred_element_type=jnp.float32)).astype(jnp.bfloat16)
            part = jnp.dot(hidden, second[quarter], preferred_element_type=jnp.float32).astype(jnp.bfloat16)
            part = lax.optimization_barrier(part)
            total = total + part.astype(jnp.float32)
        return total
    outputs = lax.map(run, (per_expert, w_in_e, w_out_e))
    back = outputs.reshape(EXPERTS, N_DP, CAP, D).transpose(1, 0, 2, 3).reshape(-1, D)
    expert_out = back[flat_place].reshape(PAIRS, SEQ, D)
    router_logits = jnp.dot(normed.reshape(-1, D), router, preferred_element_type=jnp.float32)
    gate = jax.nn.sigmoid(lax.optimization_barrier(jnp.sum(router_logits * onehot.reshape(-1, EXPERTS).astype(jnp.float32), axis=-1)))
    mixed = (tokens.astype(jnp.float32) + gate.reshape(PAIRS, SEQ, 1) * expert_out).astype(jnp.bfloat16)
    pooled = pool(mixed, out_gain, pool_query)
    emb = jnp.dot(pooled.reshape(-1, D), proj, preferred_element_type=jnp.float32).reshape(PAIRS, 2, D)
    loss, d_emb = contrast(emb, labels, logit_scale)
    flat_d = d_emb.reshape(-1, D)
    d_pooled = jnp.dot(flat_d, proj.astype(jnp.float32).T, precision=lax.Precision.HIGHEST).reshape(PAIRS, 2, D)
    grad_proj = jnp.dot(pooled.reshape(-1, D).astype(jnp.float32).T, flat_d, precision=lax.Precision.HIGHEST)
    return (mixed, d_pooled, grad_proj, loss)
```

```python
import functools
import math

import jax
import jax.numpy as jnp
from jax import lax
from jax.experimental import pallas as pl
from jax.experimental.pallas import tpu as pltpu
from jax.sharding import PartitionSpec as P

HEADS = 16
IMG_TOK = 256
SPLIT = 4
HEAD_DIM = 80
F32 = jnp.float32
BF16 = jnp.bfloat16
VMEM = pl.BlockSpec(memory_space=pltpu.VMEM)
SMEM = pl.BlockSpec(memory_space=pltpu.SMEM)


def iota(shape, dim):
    return lax.broadcasted_iota(jnp.int32, shape, dim)


def dot(a, b, contract=((1,), (0,)), precision=None):
    return lax.dot_general(
        a, b, (contract, ((), ())), precision=precision, preferred_element_type=F32
    )


def split3(values):
    high = values.astype(BF16)
    rest = values - high.astype(F32)
    middle = rest.astype(BF16)
    low = (rest - middle.astype(F32)).astype(BF16)
    return high, middle, low


def layer_norm(values, gain):
    mean = jnp.mean(values, axis=-1, keepdims=True)
    centered = values - mean
    var = jnp.mean(centered * centered, axis=-1, keepdims=True)
    return centered * lax.rsqrt(var + 1e-06) * gain


def dispatch_kernel(experts, cap, mine_ref, ids_ref, tokens_ref, *outs):
    chunks, place_ref = outs[:experts], outs[experts]
    rows = tokens_ref.shape[0]
    ids = ids_ref[...]
    onehot = (iota((experts, rows), 0) == ids).astype(F32)
    earlier = (iota((rows, rows), 0) <= iota((rows, rows), 1)).astype(F32).astype(BF16)
    count = dot(onehot.astype(BF16), earlier)
    slot = jnp.sum((count - 1.0) * onehot, axis=0, keepdims=True).astype(jnp.int32)
    place = (ids ^ mine_ref[0]) * cap + slot
    place_ref[...] = place
    select = (iota((experts * cap, rows), 0) == place).astype(F32).astype(BF16)
    buffer = dot(select, tokens_ref[...]).astype(BF16)
    for k in range(experts):
        chunks[k][...] = buffer[k * cap : (k + 1) * cap]


def ffn_kernel(mine_ref, own_ref, other_ref, gain_ref, router_ref, in_a, out_a, in_b, out_b, *outs):
    kept_ref, gate_ref, sent_ref, x_ref, hidden_ref = outs
    cap = own_ref.shape[0]
    block = 256
    gain = gain_ref[...]
    own = layer_norm(own_ref[...].astype(F32), gain).astype(BF16)
    x_ref[:cap] = own
    x_ref[cap:] = layer_norm(other_ref[...].astype(F32), gain).astype(BF16)
    ff, width = out_a.shape
    for index, w_in in enumerate((in_a, in_b)):
        for at in range(0, ff, block):
            pre = dot(x_ref[...], w_in[:, at : at + block])
            hidden_ref[index, :, at : at + block] = jax.nn.gelu(pre, approximate=True).astype(BF16)
    router = router_ref[...].astype(F32)
    column = jnp.where(iota(router.shape, 0) == mine_ref[0], router, 0.0)
    column = jnp.sum(column, axis=0, keepdims=True)
    gate_ref[...] = jax.nn.sigmoid(jnp.sum(own.astype(F32) * column, axis=1, keepdims=True))
    for at in range(0, width, block):
        total = None
        for index, w_out in enumerate((out_a, out_b)):
            part = dot(hidden_ref[index], w_out[:, at : at + block]).astype(BF16).astype(F32)
            total = part if total is None else total + part
        kept_ref[:, at : at + block] = total[:cap]
        sent_ref[:, at : at + block] = total[cap:].astype(BF16)


def finish_kernel(tokens_ref, gate_ref, kept_ref, got_ref, mixed_ref):
    total = kept_ref[...] + got_ref[...].astype(F32)
    mixed_ref[...] = (tokens_ref[...].astype(F32) + gate_ref[...] * total).astype(BF16)


def combine_kernel(experts, *refs):
    label_ref, parts, rest = refs[0], refs[1 : 1 + experts], refs[1 + experts :]
    place_ref, gain_ref, query_ref, mixed_ref, pooled_ref, buffer = rest
    cap = parts[0].shape[0]
    rows, width = mixed_ref.shape
    for k, part in enumerate(parts):
        buffer[k * cap : (k + 1) * cap] = part[...]
    select = (iota((experts * cap, rows), 0) == place_ref[...]).astype(F32).astype(BF16)
    mixed = dot(select, buffer[...], ((0,), (0,)))
    mixed_ref[...] = mixed.astype(BF16)
    z = layer_norm(mixed, gain_ref[...])
    head, feature = iota((width, HEADS), 1), iota((width, HEADS), 0)
    member = (feature >= head * HEAD_DIM) & (feature < (head + 1) * HEAD_DIM)
    member = member.astype(F32).astype(BF16)
    head, feature = iota((HEADS, width), 0), iota((HEADS, width), 1)
    spread = (feature >= head * HEAD_DIM) & (feature < (head + 1) * HEAD_DIM)
    spread = spread.astype(F32).astype(BF16)
    for modal, (lower, upper) in enumerate(((0, IMG_TOK), (IMG_TOK, rows))):
        piece = z[lower:upper]
        scores = sum(dot(term, member) for term in split3(piece * query_ref[modal : modal + 1]))
        scores = scores / math.sqrt(HEAD_DIM)
        weights = jnp.exp(scores - jnp.max(scores, axis=0, keepdims=True))
        weights = weights / jnp.sum(weights, axis=0, keepdims=True)
        wide = sum(dot(term, spread) for term in split3(weights))
        pooled_ref[modal : modal + 1] = jnp.sum(wide * piece, axis=0, keepdims=True).astype(BF16)
    pooled_ref[2:4] = jnp.full((2, width), label_ref[0], jnp.int32).astype(F32).astype(BF16)


def tail_kernel(pairs, mine_ref, scale_ref, all_ref, proj_ref, grad_ref, d_pooled_ref, loss_ref):
    exact = lax.Precision.HIGHEST
    me, scale = mine_ref[0], scale_ref[0]
    source = all_ref[...]
    row, col = iota((2 * pairs, 4 * pairs), 0), iota((2 * pairs, 4 * pairs), 1)
    wanted = jnp.where(row < pairs, (row ^ me) * 4, ((row - pairs) ^ me) * 4 + 1)
    pooled = dot((col == wanted).astype(F32).astype(BF16), source).astype(BF16)
    row, col = iota((pairs, 4 * pairs), 0), iota((pairs, 4 * pairs), 1)
    labels = dot((col == (row ^ me) * 4 + 2).astype(F32).astype(BF16), source[:, :128])[:, :1]
    emb = dot(pooled, proj_ref[...])
    norm = jnp.sqrt(jnp.sum(emb * emb, axis=-1, keepdims=True) + 1e-06)
    unit = emb / norm
    image, text = unit[:pairs], unit[pairs:]
    logits = scale * dot(image, text, ((1,), (1,)), exact)
    target = (labels == iota((pairs, pairs), 1).astype(F32)).astype(F32)
    row_top = jnp.max(logits, axis=1, keepdims=True)
    row_exp = jnp.exp(logits - row_top)
    row_total = jnp.sum(row_exp, axis=1, keepdims=True)
    row_lse = jnp.log(row_total) + row_top
    col_top = jnp.max(logits, axis=0, keepdims=True)
    col_exp = jnp.exp(logits - col_top)
    col_total = jnp.sum(col_exp, axis=0, keepdims=True)
    col_lse = jnp.log(col_total) + col_top
    matched = jnp.sum(jnp.sum(logits * target, axis=1, keepdims=True), axis=0, keepdims=True)
    total = jnp.sum(row_lse, axis=0, keepdims=True) + jnp.sum(col_lse, axis=1, keepdims=True)
    loss_ref[...] = (total - 2.0 * matched) / (2.0 * pairs)
    grad = scale * (row_exp / row_total + col_exp / col_total - 2.0 * target) / (2.0 * pairs)
    d_image = dot(grad, text, precision=exact)
    d_text = dot(grad, image, ((0,), (0,)), exact)
    d_unit = jnp.concatenate([d_image, d_text], axis=0)
    d_emb = (d_unit - unit * jnp.sum(unit * d_unit, axis=-1, keepdims=True)) / norm
    row = iota(d_emb.shape, 0)
    for modal in range(2):
        own = jnp.sum(jnp.where(row == me + modal * pairs, d_emb, 0.0), axis=0, keepdims=True)
        back = sum(dot(term, proj_ref[...], ((1,), (1,))) for term in split3(own))
        d_pooled_ref[modal : modal + 1] = back
    terms = jnp.concatenate(split3(d_emb), axis=0)
    thrice = jnp.concatenate([pooled] * 3, axis=0)
    block = 256
    for at in range(0, pooled.shape[1], block):
        grad_ref[at : at + block] = dot(thrice[:, at : at + block], terms, ((0,), (0,)))


def call(kernel, name, outs, specs, limit, scratch=()):
    return pl.pallas_call(
        kernel,
        out_shape=[jax.ShapeDtypeStruct(*o) for o in outs],
        in_specs=specs,
        out_specs=[VMEM] * len(outs),
        scratch_shapes=list(scratch),
        compiler_params=pltpu.CompilerParams(vmem_limit_bytes=limit * 1024 * 1024),
        cost_estimate=pl.CostEstimate(flops=0, bytes_accessed=0, transcendentals=0),
        name=name,
    )


def after(values, *others):
    return lax.optimization_barrier((values,) + others)[0]


def on_device(
    tokens, route, labels, moe_gain, router, w_in, w_out, out_gain, pool_query, proj, logit_scale
):
    count, length, width = tokens.shape
    rows = count * length
    devices = lax.axis_size("dp")
    experts = devices // SPLIT
    capacity = SPLIT * (3 * rows // (8 * experts) + 1)
    cap = -(-capacity // 16) * 16
    ff = w_in.shape[2]
    me = lax.axis_index("dp").astype(jnp.int32)
    mine = (me // SPLIT).reshape(1)

    def swap(values, bits):
        return lax.ppermute(values, "dp", [(i, i ^ bits) for i in range(devices)])

    weights = [w_in[0], w_out[0]]
    weights = weights + [swap(w, 1) for w in weights]
    *chunks, place = call(
        functools.partial(dispatch_kernel, experts, cap),
        "dispatch",
        [((cap, width), BF16)] * experts + [((1, rows), jnp.int32)],
        [SMEM] + [VMEM] * 2,
        8,
    )(mine, route.reshape(1, rows), tokens.reshape(rows, width))
    held = {k: swap(chunks[k], SPLIT * k) for k in range(1, min(experts, 3))}
    held[0] = chunks[0]
    parts = []
    for k in range(experts):
        if k > 2:
            held[k] = swap(after(chunks[k], held[k - 1], parts[0][2]), SPLIT * k)
        partner = swap(after(held[k], parts[(k - 1) // 2][2]) if k % 2 else held[k], 2)
        parts.append(
            call(
                ffn_kernel,
                "ffn",
                [((cap, width), F32), ((cap, 1), F32), ((cap, width), BF16)],
                [SMEM] + [VMEM] * 8,
                20,
                [pltpu.VMEM((2 * cap, width), BF16), pltpu.VMEM((2, 2 * cap, ff), BF16)],
            )(
                mine,
                held[k],
                after(partner, parts[-1][2]) if k else partner,
                moe_gain.reshape(1, width),
                router.T,
                *weights,
            )
        )
    ready, result = {}, parts[-1][2]
    for k in list(range(1, experts)) + [0]:
        kept, gate, leave = parts[k]
        got = swap(leave if k else after(leave, parts[-1][2]), 2)
        (result,) = call(finish_kernel, "finish", [((cap, width), BF16)], [VMEM] * 4, 4)(
            held[k], gate, after(kept, result), got
        )
        ready[k] = swap(result, SPLIT * k) if k else result
    mixed, pooled = call(
        functools.partial(combine_kernel, experts),
        "combine",
        [((rows, width), BF16), ((4, width), BF16)],
        [SMEM] + [VMEM] * (3 + experts),
        20,
        [pltpu.VMEM((experts * cap, width), BF16)],
    )(
        labels,
        *[ready[k] for k in range(experts)],
        place,
        out_gain.reshape(1, width),
        pool_query.reshape(2, width),
    )
    bits = 1
    while bits < devices:
        pooled = jnp.concatenate([pooled, swap(pooled, bits)], axis=0)
        bits = bits * 2
    grad_proj, d_pooled, loss = call(
        functools.partial(tail_kernel, devices),
        "contrast",
        [((width, width), F32), ((2, width), F32), ((1, 1), F32)],
        [SMEM] * 2 + [VMEM] * 2,
        24,
    )(me.reshape(1), logit_scale, pooled, proj)
    return (
        mixed.reshape(count, length, width),
        d_pooled.reshape(count, 2, width),
        grad_proj,
        loss.reshape(1),
    )


def solution(mesh):
    placed = (
        P(("groups", "dp"), None, None),
        P(("groups", "dp"), None, None),
        P(("groups", "dp")),
        P(),
        P(),
        P("dp", None, None),
        P("dp", None, None),
        P(),
        P(),
        P(),
        P(),
    )
    return jax.shard_map(
        on_device,
        mesh=mesh,
        in_specs=placed,
        out_specs=(
            P(("groups", "dp"), None, None),
            P(("groups", "dp"), None, None),
            P("groups", None),
            P("groups"),
        ),
        check_vma=False,
    )
```

```python
import functools
import math

import jax
import jax.numpy as jnp
from jax import lax
from jax.experimental import pallas as pl
from jax.experimental.pallas import tpu as pltpu
from jax.sharding import PartitionSpec as P

HEADS = 16
IMG_TOK = 256
SPLIT = 4
HEAD_DIM = 80
TILE = 256
F32 = jnp.float32
BF16 = jnp.bfloat16
VMEM = pl.BlockSpec(memory_space=pltpu.VMEM)
SMEM = pl.BlockSpec(memory_space=pltpu.SMEM)
ANY = pl.BlockSpec(memory_space=pl.ANY)
FIRST = 20_000_000_000


def iota(shape, dim):
    return lax.broadcasted_iota(jnp.int32, shape, dim)


def dot(a, b, contract=((1,), (0,)), precision=None):
    return lax.dot_general(
        a, b, (contract, ((), ())), precision=precision, preferred_element_type=F32
    )


def split3(values):
    high = values.astype(BF16)
    rest = values - high.astype(F32)
    middle = rest.astype(BF16)
    low = (rest - middle.astype(F32)).astype(BF16)
    return high, middle, low


def layer_norm(values, gain):
    mean = jnp.mean(values, axis=-1, keepdims=True)
    centered = values - mean
    var = jnp.mean(centered * centered, axis=-1, keepdims=True)
    return centered * lax.rsqrt(var + 1e-06) * gain


def dispatch_kernel(experts, cap, mine_ref, ids_ref, tokens_ref, *outs):
    chunks, place_ref = outs[:experts], outs[experts]
    rows = tokens_ref.shape[0]
    ids = ids_ref[...]
    onehot = (iota((experts, rows), 0) == ids).astype(F32)
    earlier = (iota((rows, rows), 0) <= iota((rows, rows), 1)).astype(F32).astype(BF16)
    count = dot(onehot.astype(BF16), earlier)
    slot = jnp.sum((count - 1.0) * onehot, axis=0, keepdims=True).astype(jnp.int32)
    place = (ids ^ mine_ref[0]) * cap + slot
    place_ref[...] = place
    select = (iota((experts * cap, rows), 0) == place).astype(F32).astype(BF16)
    buffer = dot(select, tokens_ref[...]).astype(BF16)
    for k in range(experts):
        chunks[k][...] = buffer[k * cap : (k + 1) * cap]


def ffn_kernel(mine_ref, own_ref, other_ref, gain_ref, router_ref, in_a, out_a, in_b, out_b, *outs):
    kept_ref, gate_ref, *sent_refs, x_ref, hidden_ref = outs
    cap = own_ref.shape[0]
    gain = gain_ref[...]
    own = layer_norm(own_ref[...].astype(F32), gain).astype(BF16)
    x_ref[:cap] = own
    x_ref[cap:] = layer_norm(other_ref[...].astype(F32), gain).astype(BF16)
    ff, width = out_a.shape
    for index, w_in in enumerate((in_a, in_b)):
        for at in range(0, ff, TILE):
            pre = dot(x_ref[...], w_in[:, at : at + TILE])
            hidden_ref[index, :, at : at + TILE] = jax.nn.gelu(pre, approximate=True).astype(BF16)
    router = router_ref[...].astype(F32)
    column = jnp.where(iota(router.shape, 0) == mine_ref[0], router, 0.0)
    column = jnp.sum(column, axis=0, keepdims=True)
    gate_ref[...] = jax.nn.sigmoid(jnp.sum(own.astype(F32) * column, axis=1, keepdims=True))
    for at in range(0, width, TILE):
        total = None
        for index, w_out in enumerate((out_a, out_b)):
            part = dot(hidden_ref[index], w_out[:, at : at + TILE]).astype(BF16).astype(F32)
            total = part if total is None else total + part
        kept_ref[:, at : at + TILE] = total[:cap]
        for sent_ref, term in zip(sent_refs, split3(total[cap:])):
            sent_ref[:, at : at + TILE] = term


def finish_kernel(tokens_ref, gate_ref, kept_ref, *refs):
    got_refs, mixed_ref = refs[:-1], refs[-1]
    total = kept_ref[...] + sum(got_ref[...].astype(F32) for got_ref in got_refs)
    mixed_ref[...] = (tokens_ref[...].astype(F32) + gate_ref[...] * total).astype(BF16)


def chosen(place, first, many):
    return (iota((many, place.shape[1]), 0) + first == place).astype(F32).astype(BF16)


def partial_kernel(*refs):
    parts, (place_ref, sum_ref, buffer) = refs[:-3], refs[-3:]
    cap = parts[0].shape[0]
    for k, part in enumerate(parts):
        buffer[k * cap : (k + 1) * cap] = part[...]
    select = chosen(place_ref[...], cap, len(parts) * cap)
    sum_ref[...] = dot(select, buffer[...], ((0,), (0,)))


def combine_kernel(experts, *refs):
    label_ref, sum_ref, back_ref, tokens_ref, gate_ref, kept_ref, high_ref, low_ref = refs[:8]
    place_ref, gain_ref, query_ref, mixed_ref, pooled_ref, buffer = refs[8:]
    cap = back_ref.shape[0]
    rows, width = mixed_ref.shape
    finish_kernel(tokens_ref, gate_ref, kept_ref, high_ref, low_ref, buffer.at[:cap])
    buffer[cap:] = back_ref[...]
    place = place_ref[...]
    select = jnp.concatenate(
        [chosen(place, 0, cap), chosen(place, (experts - 1) * cap, cap)], axis=0
    )
    mixed = sum_ref[...] + dot(select, buffer[...], ((0,), (0,)))
    mixed_ref[...] = mixed.astype(BF16)
    z = layer_norm(mixed, gain_ref[...])
    head, feature = iota((width, HEADS), 1), iota((width, HEADS), 0)
    member = (feature >= head * HEAD_DIM) & (feature < (head + 1) * HEAD_DIM)
    member = member.astype(F32).astype(BF16)
    head, feature = iota((HEADS, width), 0), iota((HEADS, width), 1)
    spread = (feature >= head * HEAD_DIM) & (feature < (head + 1) * HEAD_DIM)
    spread = spread.astype(F32).astype(BF16)
    for modal, (lower, upper) in enumerate(((0, IMG_TOK), (IMG_TOK, rows))):
        piece = z[lower:upper]
        scores = sum(dot(term, member) for term in split3(piece * query_ref[modal : modal + 1]))
        scores = scores / math.sqrt(HEAD_DIM)
        weights = jnp.exp(scores - jnp.max(scores, axis=0, keepdims=True))
        weights = weights / jnp.sum(weights, axis=0, keepdims=True)
        wide = sum(dot(term, spread) for term in split3(weights))
        pooled_ref[modal : modal + 1] = jnp.sum(wide * piece, axis=0, keepdims=True).astype(BF16)
    pooled_ref[2:4] = jnp.full((2, width), label_ref[0], jnp.int32).astype(F32).astype(BF16)


def tail_kernel(
    pairs, mine_ref, scale_ref, all_ref, proj_ref, d_pooled_ref, loss_ref, grad_ref, store, sems
):
    exact = lax.Precision.HIGHEST
    me, scale = mine_ref[0], scale_ref[0]
    source = all_ref[...]
    row, col = iota((2 * pairs, 4 * pairs), 0), iota((2 * pairs, 4 * pairs), 1)
    wanted = jnp.where(row < pairs, (row ^ me) * 4, ((row - pairs) ^ me) * 4 + 1)
    pooled = dot((col == wanted).astype(F32).astype(BF16), source).astype(BF16)
    row, col = iota((pairs, 4 * pairs), 0), iota((pairs, 4 * pairs), 1)
    labels = dot((col == (row ^ me) * 4 + 2).astype(F32).astype(BF16), source[:, :128])[:, :1]
    emb = dot(pooled, proj_ref[...])
    norm = jnp.sqrt(jnp.sum(emb * emb, axis=-1, keepdims=True) + 1e-06)
    unit = emb / norm
    image, text = unit[:pairs], unit[pairs:]
    logits = scale * dot(image, text, ((1,), (1,)), exact)
    target = (labels == iota((pairs, pairs), 1).astype(F32)).astype(F32)
    row_top = jnp.max(logits, axis=1, keepdims=True)
    row_exp = jnp.exp(logits - row_top)
    row_total = jnp.sum(row_exp, axis=1, keepdims=True)
    row_lse = jnp.log(row_total) + row_top
    col_top = jnp.max(logits, axis=0, keepdims=True)
    col_exp = jnp.exp(logits - col_top)
    col_total = jnp.sum(col_exp, axis=0, keepdims=True)
    col_lse = jnp.log(col_total) + col_top
    matched = jnp.sum(jnp.sum(logits * target, axis=1, keepdims=True), axis=0, keepdims=True)
    total = jnp.sum(row_lse, axis=0, keepdims=True) + jnp.sum(col_lse, axis=1, keepdims=True)
    loss_ref[...] = (total - 2.0 * matched) / (2.0 * pairs)
    grad = scale * (row_exp / row_total + col_exp / col_total - 2.0 * target) / (2.0 * pairs)
    d_image = dot(grad, text, precision=exact)
    d_text = dot(grad, image, ((0,), (0,)), exact)
    d_unit = jnp.concatenate([d_image, d_text], axis=0)
    d_emb = (d_unit - unit * jnp.sum(unit * d_unit, axis=-1, keepdims=True)) / norm
    terms = jnp.concatenate(split3(d_emb), axis=0)
    thrice = jnp.concatenate([pooled] * 3, axis=0)
    copies = []
    for at in range(0, pooled.shape[1], TILE):
        store[at : at + TILE] = dot(thrice[:, at : at + TILE], terms, ((0,), (0,)))
        copies.append(
            pltpu.make_async_copy(
                store.at[at : at + TILE], grad_ref.at[at : at + TILE], sems.at[at // TILE]
            )
        )
        copies[-1].start()
    row = iota(d_emb.shape, 0)
    own = [
        jnp.sum(jnp.where(row == me + modal * pairs, d_emb, 0.0), axis=0, keepdims=True)
        for modal in range(2)
    ]
    terms = jnp.concatenate(split3(jnp.concatenate(own, axis=0)), axis=0)
    back = dot(terms, proj_ref[...], ((1,), (1,)))
    d_pooled_ref[...] = back[0:2] + back[2:4] + back[4:6]
    for copy in copies:
        copy.wait()


def call(kernel, name, outs, specs, limit, scratch=(), flops=0, in_hbm=0):
    return pl.pallas_call(
        kernel,
        out_shape=[jax.ShapeDtypeStruct(*o) for o in outs],
        in_specs=specs,
        out_specs=[VMEM] * (len(outs) - in_hbm) + [ANY] * in_hbm,
        scratch_shapes=list(scratch),
        compiler_params=pltpu.CompilerParams(vmem_limit_bytes=limit * 1024 * 1024),
        cost_estimate=pl.CostEstimate(flops=flops, bytes_accessed=0, transcendentals=0),
        name=name,
    )


def after(values, *others):
    return lax.optimization_barrier((values,) + others)[0]


def on_device(
    tokens, route, labels, moe_gain, router, w_in, w_out, out_gain, pool_query, proj, logit_scale
):
    count, length, width = tokens.shape
    rows = count * length
    devices = lax.axis_size("dp")
    experts = devices // SPLIT
    capacity = SPLIT * (3 * rows // (8 * experts) + 1)
    cap = -(-capacity // 16) * 16
    ff = w_in.shape[2]
    me = lax.axis_index("dp").astype(jnp.int32)
    mine = (me // SPLIT).reshape(1)

    def swap(values, bits):
        return lax.ppermute(values, "dp", [(i, i ^ bits) for i in range(devices)])

    weights = [w_in[0], w_out[0]]
    weights = weights + [swap(w, 1) for w in weights]
    *chunks, place = call(
        functools.partial(dispatch_kernel, experts, cap),
        "dispatch",
        [((cap, width), BF16)] * experts + [((1, rows), jnp.int32)],
        [SMEM] + [VMEM] * 2,
        8,
        flops=FIRST,
    )(mine, route.reshape(1, rows), tokens.reshape(rows, width))
    held = {k: swap(chunks[k], SPLIT * k) for k in range(1, min(experts, 3))}
    held[0] = chunks[0]
    parts = []
    for k in range(experts):
        if k > 2:
            held[k] = swap(after(chunks[k], held[k - 1], parts[0][2]), SPLIT * k)
        partner = swap(after(held[k], parts[(k - 1) // 2][2]) if k % 2 else held[k], 2)
        parts.append(
            call(
                ffn_kernel,
                "ffn",
                [((cap, width), F32), ((cap, 1), F32)] + [((cap, width), BF16)] * (1 if k else 2),
                [SMEM] + [VMEM] * 8,
                20,
                [pltpu.VMEM((2 * cap, width), BF16), pltpu.VMEM((2, 2 * cap, ff), BF16)],
            )(
                mine,
                held[k],
                after(partner, parts[-1][2]) if k else partner,
                moe_gain.reshape(1, width),
                router.T,
                *weights,
            )
        )
    ready, result = {}, parts[-1][2]
    for k in range(1, experts):
        kept, gate, leave = parts[k]
        (result,) = call(finish_kernel, "finish", [((cap, width), BF16)], [VMEM] * 4, 4)(
            held[k], gate, after(kept, result), swap(leave, 2)
        )
        ready[k] = swap(result, SPLIT * k)
    kept, gate, *leave = parts[0]
    got = [swap(after(term, result), 2) for term in leave]
    (partial,) = call(
        partial_kernel,
        "partial",
        [((rows, width), F32)],
        [VMEM] * (experts - 1),
        8,
        [pltpu.VMEM(((experts - 2) * cap, width), BF16)],
    )(*[ready[k] for k in range(1, experts - 1)], place)
    mixed, pooled = call(
        functools.partial(combine_kernel, experts),
        "combine",
        [((rows, width), BF16), ((4, width), BF16)],
        [SMEM] + [VMEM] * 10,
        20,
        [pltpu.VMEM((2 * cap, width), BF16)],
    )(
        labels,
        partial,
        ready[experts - 1],
        held[0],
        gate,
        kept,
        *got,
        place,
        out_gain.reshape(1, width),
        pool_query.reshape(2, width),
    )
    bits = 1
    while bits < devices:
        pooled = jnp.concatenate([pooled, swap(pooled, bits)], axis=0)
        bits = bits * 2
    d_pooled, loss, grad_proj = call(
        functools.partial(tail_kernel, devices),
        "contrast",
        [((2, width), F32), ((1, 1), F32), ((width, width), F32)],
        [SMEM] * 2 + [VMEM] * 2,
        24,
        [pltpu.VMEM((width, width), F32), pltpu.SemaphoreType.DMA((-(-width // TILE),))],
        in_hbm=1,
    )(me.reshape(1), logit_scale, pooled, proj)
    return (
        mixed.reshape(count, length, width),
        d_pooled.reshape(count, 2, width),
        grad_proj,
        loss.reshape(1),
    )


def solution(mesh):
    placed = (
        P(("groups", "dp"), None, None),
        P(("groups", "dp"), None, None),
        P(("groups", "dp")),
        P(),
        P(),
        P("dp", None, None),
        P("dp", None, None),
        P(),
        P(),
        P(),
        P(),
    )
    return jax.shard_map(
        on_device,
        mesh=mesh,
        in_specs=placed,
        out_specs=(
            P(("groups", "dp"), None, None),
            P(("groups", "dp"), None, None),
            P("groups", None),
            P("groups"),
        ),
        check_vma=False,
    )
```

```python
import functools
import math

import jax
import jax.numpy as jnp
from jax import lax
from jax.experimental import pallas as pl
from jax.experimental.pallas import tpu as pltpu
from jax.sharding import PartitionSpec as P

HEADS = 16
IMG_TOK = 256
SPLIT = 4
HEAD_DIM = 80
TILE = 256
F32 = jnp.float32
BF16 = jnp.bfloat16
VMEM = pl.BlockSpec(memory_space=pltpu.VMEM)
SMEM = pl.BlockSpec(memory_space=pltpu.SMEM)
ANY = pl.BlockSpec(memory_space=pl.ANY)
FIRST = 20_000_000_000


def iota(shape, dim):
    return lax.broadcasted_iota(jnp.int32, shape, dim)


def dot(a, b, contract=((1,), (0,)), precision=None):
    return lax.dot_general(
        a, b, (contract, ((), ())), precision=precision, preferred_element_type=F32
    )


def split3(values):
    high = values.astype(BF16)
    rest = values - high.astype(F32)
    middle = rest.astype(BF16)
    low = (rest - middle.astype(F32)).astype(BF16)
    return high, middle, low


def layer_norm(values, gain):
    mean = jnp.mean(values, axis=-1, keepdims=True)
    centered = values - mean
    var = jnp.mean(centered * centered, axis=-1, keepdims=True)
    return centered * lax.rsqrt(var + 1e-06) * gain


def dispatch_kernel(experts, cap, mine_ref, ids_ref, tokens_ref, *outs):
    chunks, place_ref = outs[:experts], outs[experts]
    rows = tokens_ref.shape[0]
    ids = ids_ref[...]
    onehot = (iota((experts, rows), 0) == ids).astype(F32)
    earlier = (iota((rows, rows), 0) <= iota((rows, rows), 1)).astype(F32).astype(BF16)
    count = dot(onehot.astype(BF16), earlier)
    slot = jnp.sum((count - 1.0) * onehot, axis=0, keepdims=True).astype(jnp.int32)
    place = (ids ^ mine_ref[0]) * cap + slot
    place_ref[...] = place
    select = (iota((experts * cap, rows), 0) == place).astype(F32).astype(BF16)
    buffer = dot(select, tokens_ref[...]).astype(BF16)
    for k in range(experts):
        chunks[k][...] = buffer[k * cap : (k + 1) * cap]


def ffn_kernel(mine_ref, own_ref, other_ref, gain_ref, router_ref, in_a, out_a, in_b, out_b, *outs):
    kept_ref, gate_ref, *sent_refs, x_ref, hidden_ref = outs
    cap = own_ref.shape[0]
    gain = gain_ref[...]
    own = layer_norm(own_ref[...].astype(F32), gain).astype(BF16)
    x_ref[:cap] = own
    x_ref[cap:] = layer_norm(other_ref[...].astype(F32), gain).astype(BF16)
    ff, width = out_a.shape
    for index, w_in in enumerate((in_a, in_b)):
        for at in range(0, ff, TILE):
            pre = dot(x_ref[...], w_in[:, at : at + TILE])
            hidden_ref[index, :, at : at + TILE] = jax.nn.gelu(pre, approximate=True).astype(BF16)
    router = router_ref[...].astype(F32)
    column = jnp.where(iota(router.shape, 0) == mine_ref[0], router, 0.0)
    column = jnp.sum(column, axis=0, keepdims=True)
    gate_ref[...] = jax.nn.sigmoid(jnp.sum(own.astype(F32) * column, axis=1, keepdims=True))
    for at in range(0, width, TILE):
        total = None
        for index, w_out in enumerate((out_a, out_b)):
            part = dot(hidden_ref[index], w_out[:, at : at + TILE]).astype(BF16).astype(F32)
            total = part if total is None else total + part
        kept_ref[:, at : at + TILE] = total[:cap]
        for sent_ref, term in zip(sent_refs, split3(total[cap:])):
            sent_ref[:, at : at + TILE] = term


def finish_kernel(tokens_ref, gate_ref, kept_ref, *refs):
    got_refs, mixed_ref = refs[:-1], refs[-1]
    total = kept_ref[...] + sum(got_ref[...].astype(F32) for got_ref in got_refs)
    mixed_ref[...] = (tokens_ref[...].astype(F32) + gate_ref[...] * total).astype(BF16)


def chosen(place, first, many):
    return (iota((many, place.shape[1]), 0) + first == place).astype(F32).astype(BF16)


def heads_of(shape):
    head, feature = iota(shape, 0), iota(shape, 1)
    return (feature >= head * HEAD_DIM) & (feature < (head + 1) * HEAD_DIM)


def partial_kernel(early, query_ref, place_ref, *refs):
    parts, sum_ref, rows_ref, buffer = refs[:-3], *refs[-3:]
    cap, width = parts[0].shape
    for at, part_ref in enumerate(parts):
        buffer[at * cap : (at + 1) * cap] = part_ref[...]
    place = place_ref[...]
    select = jnp.concatenate([chosen(place, k * cap, cap) for k in early], axis=0)
    sum_ref[...] = dot(select, buffer[...], ((0,), (0,)))
    feature = iota((1, width), 1)
    inner = feature - HEAD_DIM * sum(
        (feature >= h * HEAD_DIM).astype(jnp.int32) for h in range(1, HEADS)
    )
    spread = (iota((HEAD_DIM, width), 0) == inner).astype(F32).astype(BF16)
    for modal in range(2):
        wide = sum(dot(term, spread) for term in split3(query_ref[modal]))
        wide = jnp.where(heads_of((HEADS, width)), wide, 0.0)
        rows_ref[modal : modal + 1] = jnp.sum(wide, axis=0, keepdims=True)


def combine_kernel(late, *refs):
    label_ref, sum_ref, tokens_ref, gate_ref, kept_ref, high_ref, low_ref, place_ref = refs[:8]
    gain_ref, query_ref, *backs, mixed_ref, pooled_ref, buffer = refs[8:]
    cap = kept_ref.shape[0]
    rows, width = mixed_ref.shape
    finish_kernel(tokens_ref, gate_ref, kept_ref, high_ref, low_ref, buffer.at[:cap])
    for at, back_ref in enumerate(backs):
        buffer[(at + 1) * cap : (at + 2) * cap] = back_ref[...]
    place = place_ref[...]
    select = jnp.concatenate([chosen(place, k * cap, cap) for k in [0] + late], axis=0)
    mixed = sum_ref[...] + dot(select, buffer[...], ((0,), (0,)))
    mixed_ref[...] = mixed.astype(BF16)
    z = layer_norm(mixed, gain_ref[...])
    head, feature = iota((width, HEADS), 1), iota((width, HEADS), 0)
    member = (feature >= head * HEAD_DIM) & (feature < (head + 1) * HEAD_DIM)
    member = member.astype(F32).astype(BF16)
    spread = heads_of((HEADS, width)).astype(F32).astype(BF16)
    for modal, (lower, upper) in enumerate(((0, IMG_TOK), (IMG_TOK, rows))):
        piece = z[lower:upper]
        scores = sum(dot(term, member) for term in split3(piece * query_ref[modal : modal + 1]))
        scores = scores / math.sqrt(HEAD_DIM)
        weights = jnp.exp(scores - jnp.max(scores, axis=0, keepdims=True))
        weights = weights / jnp.sum(weights, axis=0, keepdims=True)
        wide = sum(dot(term, spread) for term in split3(weights))
        pooled_ref[modal : modal + 1] = jnp.sum(wide * piece, axis=0, keepdims=True).astype(BF16)
    pooled_ref[2:4] = jnp.full((2, width), label_ref[0], jnp.int32).astype(F32).astype(BF16)


def tail_kernel(
    pairs, mine_ref, scale_ref, proj_ref, *refs
):
    pieces, (d_pooled_ref, loss_ref, grad_ref, store, sems) = refs[:-5], refs[-5:]
    exact = lax.Precision.HIGHEST
    me, scale = mine_ref[0], scale_ref[0]
    at, pooled, labels = 0, 0.0, 0.0
    for piece in pieces:
        many = piece.shape[0]
        row, col = iota((2 * pairs, many), 0), iota((2 * pairs, many), 1) + at
        wanted = jnp.where(row < pairs, (row ^ me) * 4, ((row - pairs) ^ me) * 4 + 1)
        pooled = pooled + dot((col == wanted).astype(F32).astype(BF16), piece[...])
        row, col = iota((pairs, many), 0), iota((pairs, many), 1) + at
        wanted = (col == (row ^ me) * 4 + 2).astype(F32).astype(BF16)
        labels = labels + dot(wanted, piece[:, :128])
        at = at + many
    pooled, labels = pooled.astype(BF16), labels[:, :1]
    emb = dot(pooled, proj_ref[...])
    norm = jnp.sqrt(jnp.sum(emb * emb, axis=-1, keepdims=True) + 1e-06)
    unit = emb / norm
    image, text = unit[:pairs], unit[pairs:]
    logits = scale * dot(image, text, ((1,), (1,)), exact)
    target = (labels == iota((pairs, pairs), 1).astype(F32)).astype(F32)
    row_top = jnp.max(logits, axis=1, keepdims=True)
    row_exp = jnp.exp(logits - row_top)
    row_total = jnp.sum(row_exp, axis=1, keepdims=True)
    row_lse = jnp.log(row_total) + row_top
    col_top = jnp.max(logits, axis=0, keepdims=True)
    col_exp = jnp.exp(logits - col_top)
    col_total = jnp.sum(col_exp, axis=0, keepdims=True)
    col_lse = jnp.log(col_total) + col_top
    matched = jnp.sum(jnp.sum(logits * target, axis=1, keepdims=True), axis=0, keepdims=True)
    total = jnp.sum(row_lse, axis=0, keepdims=True) + jnp.sum(col_lse, axis=1, keepdims=True)
    loss_ref[...] = (total - 2.0 * matched) / (2.0 * pairs)
    grad = scale * (row_exp / row_total + col_exp / col_total - 2.0 * target) / (2.0 * pairs)
    d_image = dot(grad, text, precision=exact)
    d_text = dot(grad, image, ((0,), (0,)), exact)
    d_unit = jnp.concatenate([d_image, d_text], axis=0)
    d_emb = (d_unit - unit * jnp.sum(unit * d_unit, axis=-1, keepdims=True)) / norm
    terms = jnp.concatenate(split3(d_emb), axis=0)
    thrice = jnp.concatenate([pooled] * 3, axis=0)
    copies = []
    for at in range(0, pooled.shape[1], TILE):
        store[at : at + TILE] = dot(thrice[:, at : at + TILE], terms, ((0,), (0,)))
        copies.append(
            pltpu.make_async_copy(
                store.at[at : at + TILE], grad_ref.at[at : at + TILE], sems.at[at // TILE]
            )
        )
        copies[-1].start()
    row = iota(d_emb.shape, 0)
    own = [
        jnp.sum(jnp.where(row == me + modal * pairs, d_emb, 0.0), axis=0, keepdims=True)
        for modal in range(2)
    ]
    terms = jnp.concatenate(split3(jnp.concatenate(own, axis=0)), axis=0)
    back = dot(terms, proj_ref[...], ((1,), (1,)))
    d_pooled_ref[...] = back[0:2] + back[2:4] + back[4:6]
    for copy in copies:
        copy.wait()


def call(kernel, name, outs, specs, limit, scratch=(), flops=0, in_hbm=0):
    return pl.pallas_call(
        kernel,
        out_shape=[jax.ShapeDtypeStruct(*o) for o in outs],
        in_specs=specs,
        out_specs=[VMEM] * (len(outs) - in_hbm) + [ANY] * in_hbm,
        scratch_shapes=list(scratch),
        compiler_params=pltpu.CompilerParams(vmem_limit_bytes=limit * 1024 * 1024),
        cost_estimate=pl.CostEstimate(flops=flops, bytes_accessed=0, transcendentals=0),
        name=name,
    )


def after(values, *others):
    return lax.optimization_barrier((values,) + others)[0] if others else values


def on_device(
    tokens, route, labels, moe_gain, router, w_in, w_out, out_gain, pool_query, proj, logit_scale
):
    count, length, width = tokens.shape
    rows = count * length
    devices = lax.axis_size("dp")
    experts = devices // SPLIT
    capacity = SPLIT * (3 * rows // (8 * experts) + 1)
    cap = -(-capacity // 16) * 16
    ff = w_in.shape[2]
    me = lax.axis_index("dp").astype(jnp.int32)
    mine = (me // SPLIT).reshape(1)

    def swap(values, bits):
        return lax.ppermute(values, "dp", [(i, i ^ bits) for i in range(devices)])

    weights = [w_in[0], w_out[0]]
    weights = weights + [swap(w, 1) for w in weights]
    *chunks, place = call(
        functools.partial(dispatch_kernel, experts, cap),
        "dispatch",
        [((cap, width), BF16)] * experts + [((1, rows), jnp.int32)],
        [SMEM] + [VMEM] * 2,
        8,
        flops=FIRST,
    )(mine, route.reshape(1, rows), tokens.reshape(rows, width))
    held = {0: chunks[0]}
    for k in range(1, min(experts, 3)):
        held[k] = swap(chunks[k], SPLIT * k)
    parts, done, final = {}, [], {}

    def finish(k, early=None):
        kept, gate, leave = parts[k]
        (final[k],) = call(finish_kernel, "finish", [((cap, width), BF16)], [VMEM] * 4, 4)(
            held[k],
            gate,
            kept if early is None else after(kept, early),
            swap(leave, 2),
        )

    for k in range(experts):
        waits = done[-1:]
        if k > 2:
            held[k] = swap(after(chunks[k], done[0], held[k - 1]), SPLIT * k)
        if k < 2 and k + 1 < experts:
            waits = waits + [held[k + 1]]
        partner = swap(after(held[k], done[k - 1 if k > 2 else 0]) if k > 1 else held[k], 2)
        if k == 3:
            finish(2, early=partner)
            waits = waits + [final[2]]
        kept, gate, *leave = call(
            ffn_kernel,
            "ffn",
            [((cap, width), F32), ((cap, 1), F32)] + [((cap, width), BF16)] * (1 if k else 2),
            [SMEM] + [VMEM] * 8,
            20,
            [pltpu.VMEM((2 * cap, width), BF16), pltpu.VMEM((2, 2 * cap, ff), BF16)],
        )(
            mine,
            held[k],
            after(partner, *waits),
            moe_gain.reshape(1, width),
            router.T,
            *weights,
        )
        parts[k] = (kept, gate, leave[0] if k else leave)
        done.append(leave[0])
    finish(1)
    early = [1, 2]
    partial, query = call(
        functools.partial(partial_kernel, early),
        "partial",
        [((rows, width), F32), ((2, width), F32)],
        [VMEM] * 4,
        8,
        [pltpu.VMEM((2 * cap, width), BF16)],
    )(pool_query, place, *[swap(final[k], SPLIT * k) for k in early])
    for k in range(3, experts):
        finish(k, early=partial)
    result = final[experts - 1]
    kept, gate, leave = parts[0]
    got = [swap(after(term, result), 2) for term in leave]
    late = list(range(3, experts))
    mixed, pooled = call(
        functools.partial(combine_kernel, late),
        "combine",
        [((rows, width), BF16), ((4, width), BF16)],
        [SMEM] + [VMEM] * (9 + len(late)),
        20,
        [pltpu.VMEM(((1 + len(late)) * cap, width), BF16)],
    )(
        labels,
        partial,
        held[0],
        gate,
        kept,
        *got,
        place,
        out_gain.reshape(1, width),
        query,
        *[swap(final[k], SPLIT * k) for k in late],
    )
    pieces, bits = [pooled], 1
    while bits < devices:
        pieces.append(swap(jnp.concatenate(pieces, axis=0), bits))
        bits = bits * 2
    d_pooled, loss, grad_proj = call(
        functools.partial(tail_kernel, devices),
        "contrast",
        [((2, width), F32), ((1, 1), F32), ((width, width), F32)],
        [SMEM] * 2 + [VMEM] * (1 + len(pieces)),
        24,
        [pltpu.VMEM((width, width), F32), pltpu.SemaphoreType.DMA((-(-width // TILE),))],
        in_hbm=1,
    )(me.reshape(1), logit_scale, proj, *pieces)
    return (
        mixed.reshape(count, length, width),
        d_pooled.reshape(count, 2, width),
        grad_proj,
        loss.reshape(1),
    )


def solution(mesh):
    placed = (
        P(("groups", "dp"), None, None),
        P(("groups", "dp"), None, None),
        P(("groups", "dp")),
        P(),
        P(),
        P("dp", None, None),
        P("dp", None, None),
        P(),
        P(),
        P(),
        P(),
    )
    return jax.shard_map(
        on_device,
        mesh=mesh,
        in_specs=placed,
        out_specs=(
            P(("groups", "dp"), None, None),
            P(("groups", "dp"), None, None),
            P("groups", None),
            P("groups"),
        ),
        check_vma=False,
    )
```

```python
import functools
import math

import jax
import jax.numpy as jnp
from jax import lax
from jax.experimental import pallas as pl
from jax.experimental.pallas import tpu as pltpu
from jax.sharding import PartitionSpec as P

HEADS = 16
IMG_TOK = 256
SPLIT = 4
HEAD_DIM = 80
TILE = 256
F32 = jnp.float32
BF16 = jnp.bfloat16
VMEM = pl.BlockSpec(memory_space=pltpu.VMEM)
SMEM = pl.BlockSpec(memory_space=pltpu.SMEM)
ANY = pl.BlockSpec(memory_space=pl.ANY)
FIRST = 20_000_000_000


def iota(shape, dim):
    return lax.broadcasted_iota(jnp.int32, shape, dim)


def dot(a, b, contract=((1,), (0,)), precision=None):
    return lax.dot_general(
        a, b, (contract, ((), ())), precision=precision, preferred_element_type=F32
    )


def split3(values):
    high = values.astype(BF16)
    rest = values - high.astype(F32)
    middle = rest.astype(BF16)
    low = (rest - middle.astype(F32)).astype(BF16)
    return high, middle, low


def layer_norm(values, gain):
    mean = jnp.mean(values, axis=-1, keepdims=True)
    centered = values - mean
    var = jnp.mean(centered * centered, axis=-1, keepdims=True)
    return centered * lax.rsqrt(var + 1e-06) * gain


def dispatch_kernel(experts, cap, mine_ref, ids_ref, tokens_ref, *outs):
    chunks, place_ref = outs[:experts], outs[experts]
    rows = tokens_ref.shape[0]
    ids = ids_ref[...]
    onehot = (iota((experts, rows), 0) == ids).astype(F32)
    earlier = (iota((rows, rows), 0) <= iota((rows, rows), 1)).astype(F32).astype(BF16)
    count = dot(onehot.astype(BF16), earlier)
    slot = jnp.sum((count - 1.0) * onehot, axis=0, keepdims=True).astype(jnp.int32)
    place = (ids ^ (mine_ref[0] // SPLIT)) * cap + slot
    place_ref[...] = place
    select = (iota((experts * cap, rows), 0) == place).astype(F32).astype(BF16)
    buffer = dot(select, tokens_ref[...]).astype(BF16)
    for k in range(experts):
        chunks[k][...] = buffer[k * cap : (k + 1) * cap]


def ffn_kernel(own, mine_ref, rows_ref, gain_ref, router_ref, in_a, out_a, in_b, out_b, *outs):
    *outs, x_ref, hidden_ref = outs
    normed = layer_norm(rows_ref[...].astype(F32), gain_ref[...]).astype(BF16)
    x_ref[...] = normed
    ff, width = out_a.shape
    for index, w_in in enumerate((in_a, in_b)):
        for at in range(0, ff, TILE):
            pre = dot(x_ref[...], w_in[:, at : at + TILE])
            hidden_ref[index, :, at : at + TILE] = jax.nn.gelu(pre, approximate=True).astype(BF16)
    if own:
        router = router_ref[...].astype(F32)
        column = jnp.where(iota(router.shape, 0) == mine_ref[0] // SPLIT, router, 0.0)
        column = jnp.sum(column, axis=0, keepdims=True)
        gate = jnp.sum(normed.astype(F32) * column, axis=1, keepdims=True)
        outs[1][...] = jax.nn.sigmoid(gate)
    for at in range(0, width, TILE):
        total = None
        for index, w_out in enumerate((out_a, out_b)):
            part = dot(hidden_ref[index], w_out[:, at : at + TILE]).astype(BF16).astype(F32)
            total = part if total is None else total + part
        if own:
            outs[0][:, at : at + TILE] = total
        else:
            for out_ref, term in zip(outs, split3(total)):
                out_ref[:, at : at + TILE] = term[: out_ref.shape[0]]


def finish_kernel(tokens_ref, gate_ref, kept_ref, *refs):
    got_ref, *low_refs, mixed_ref = refs
    total = kept_ref[...] + got_ref[...].astype(F32)
    for low_ref in low_refs:
        many = low_ref.shape[0]
        total = jnp.concatenate([total[:many] + low_ref[...].astype(F32), total[many:]], axis=0)
    mixed_ref[...] = (tokens_ref[...].astype(F32) + gate_ref[...] * total).astype(BF16)


def chosen(place, first, many):
    return (iota((many, place.shape[1]), 0) + first == place).astype(F32).astype(BF16)


def heads_of(shape):
    head, feature = iota(shape, 0), iota(shape, 1)
    return (feature >= head * HEAD_DIM) & (feature < (head + 1) * HEAD_DIM)


def partial_kernel(early, query_ref, place_ref, *refs):
    parts, sum_ref, rows_ref, buffer = refs[:-3], *refs[-3:]
    cap, width = parts[0].shape
    for at, part_ref in enumerate(parts):
        buffer[at * cap : (at + 1) * cap] = part_ref[...]
    place = place_ref[...]
    select = jnp.concatenate([chosen(place, k * cap, cap) for k in early], axis=0)
    sum_ref[...] = dot(select, buffer[...], ((0,), (0,)))
    feature = iota((1, width), 1)
    inner = feature - HEAD_DIM * sum(
        (feature >= h * HEAD_DIM).astype(jnp.int32) for h in range(1, HEADS)
    )
    spread = (iota((HEAD_DIM, width), 0) == inner).astype(F32).astype(BF16)
    for modal in range(2):
        wide = sum(dot(term, spread) for term in split3(query_ref[modal]))
        wide = jnp.where(heads_of((HEADS, width)), wide, 0.0)
        rows_ref[modal : modal + 1] = jnp.sum(wide, axis=0, keepdims=True)


def combine_kernel(late, *refs):
    label_ref, sum_ref, tokens_ref, gate_ref, kept_ref, high_ref, low_ref, place_ref = refs[:8]
    gain_ref, query_ref, *backs, mixed_ref, pooled_ref, buffer = refs[8:]
    cap = kept_ref.shape[0]
    rows, width = mixed_ref.shape
    finish_kernel(tokens_ref, gate_ref, kept_ref, high_ref, low_ref, buffer.at[:cap])
    for at, back_ref in enumerate(backs):
        buffer[(at + 1) * cap : (at + 2) * cap] = back_ref[...]
    place = place_ref[...]
    select = jnp.concatenate([chosen(place, k * cap, cap) for k in [0] + late], axis=0)
    mixed = sum_ref[...] + dot(select, buffer[...], ((0,), (0,)))
    mixed_ref[...] = mixed.astype(BF16)
    z = layer_norm(mixed, gain_ref[...])
    head, feature = iota((width, HEADS), 1), iota((width, HEADS), 0)
    member = (feature >= head * HEAD_DIM) & (feature < (head + 1) * HEAD_DIM)
    member = member.astype(F32).astype(BF16)
    spread = heads_of((HEADS, width)).astype(F32).astype(BF16)
    for modal, (lower, upper) in enumerate(((0, IMG_TOK), (IMG_TOK, rows))):
        piece = z[lower:upper]
        scores = sum(dot(term, member) for term in split3(piece * query_ref[modal : modal + 1]))
        scores = scores / math.sqrt(HEAD_DIM)
        weights = jnp.exp(scores - jnp.max(scores, axis=0, keepdims=True))
        weights = weights / jnp.sum(weights, axis=0, keepdims=True)
        wide = sum(dot(term, spread) for term in split3(weights))
        pooled_ref[modal : modal + 1] = jnp.sum(wide * piece, axis=0, keepdims=True).astype(BF16)
    pooled_ref[2:4] = jnp.full((2, width), label_ref[0], jnp.int32).astype(F32).astype(BF16)


def tail_kernel(
    pairs, mine_ref, scale_ref, proj_ref, *refs
):
    pieces, (d_pooled_ref, loss_ref, grad_ref, store, sems) = refs[:-5], refs[-5:]
    exact = lax.Precision.HIGHEST
    me, scale = mine_ref[0], scale_ref[0]
    at, pooled, labels = 0, 0.0, 0.0
    for piece in pieces:
        many = piece.shape[0]
        row, col = iota((2 * pairs, many), 0), iota((2 * pairs, many), 1) + at
        wanted = jnp.where(row < pairs, (row ^ me) * 4, ((row - pairs) ^ me) * 4 + 1)
        pooled = pooled + dot((col == wanted).astype(F32).astype(BF16), piece[...])
        row, col = iota((pairs, many), 0), iota((pairs, many), 1) + at
        wanted = (col == (row ^ me) * 4 + 2).astype(F32).astype(BF16)
        labels = labels + dot(wanted, piece[:, :128])
        at = at + many
    pooled, labels = pooled.astype(BF16), labels[:, :1]
    emb = dot(pooled, proj_ref[...])
    norm = jnp.sqrt(jnp.sum(emb * emb, axis=-1, keepdims=True) + 1e-06)
    unit = emb / norm
    image, text = unit[:pairs], unit[pairs:]
    logits = scale * dot(image, text, ((1,), (1,)), exact)
    target = (labels == iota((pairs, pairs), 1).astype(F32)).astype(F32)
    row_top = jnp.max(logits, axis=1, keepdims=True)
    row_exp = jnp.exp(logits - row_top)
    row_total = jnp.sum(row_exp, axis=1, keepdims=True)
    row_lse = jnp.log(row_total) + row_top
    col_top = jnp.max(logits, axis=0, keepdims=True)
    col_exp = jnp.exp(logits - col_top)
    col_total = jnp.sum(col_exp, axis=0, keepdims=True)
    col_lse = jnp.log(col_total) + col_top
    matched = jnp.sum(jnp.sum(logits * target, axis=1, keepdims=True), axis=0, keepdims=True)
    total = jnp.sum(row_lse, axis=0, keepdims=True) + jnp.sum(col_lse, axis=1, keepdims=True)
    loss_ref[...] = (total - 2.0 * matched) / (2.0 * pairs)
    grad = scale * (row_exp / row_total + col_exp / col_total - 2.0 * target) / (2.0 * pairs)
    d_image = dot(grad, text, precision=exact)
    d_text = dot(grad, image, ((0,), (0,)), exact)
    d_unit = jnp.concatenate([d_image, d_text], axis=0)
    d_emb = (d_unit - unit * jnp.sum(unit * d_unit, axis=-1, keepdims=True)) / norm
    terms = jnp.concatenate(split3(d_emb), axis=0)
    thrice = jnp.concatenate([pooled] * 3, axis=0)
    copies = []
    for at in range(0, pooled.shape[1], TILE):
        store[at : at + TILE] = dot(thrice[:, at : at + TILE], terms, ((0,), (0,)))
        copies.append(
            pltpu.make_async_copy(
                store.at[at : at + TILE], grad_ref.at[at : at + TILE], sems.at[at // TILE]
            )
        )
        copies[-1].start()
    row = iota(d_emb.shape, 0)
    own = [
        jnp.sum(jnp.where(row == me + modal * pairs, d_emb, 0.0), axis=0, keepdims=True)
        for modal in range(2)
    ]
    terms = jnp.concatenate(split3(jnp.concatenate(own, axis=0)), axis=0)
    back = dot(terms, proj_ref[...], ((1,), (1,)))
    d_pooled_ref[...] = back[0:2] + back[2:4] + back[4:6]
    for copy in copies:
        copy.wait()


def call(kernel, name, outs, specs, limit, scratch=(), flops=0, in_hbm=0):
    return pl.pallas_call(
        kernel,
        out_shape=[jax.ShapeDtypeStruct(*o) for o in outs],
        in_specs=specs,
        out_specs=[VMEM] * (len(outs) - in_hbm) + [ANY] * in_hbm,
        scratch_shapes=list(scratch),
        compiler_params=pltpu.CompilerParams(vmem_limit_bytes=limit * 1024 * 1024),
        cost_estimate=pl.CostEstimate(flops=flops, bytes_accessed=0, transcendentals=0),
        name=name,
    )


def after(values, *others):
    return lax.optimization_barrier((values,) + others)[0] if others else values


def on_device(
    tokens, route, labels, moe_gain, router, w_in, w_out, out_gain, pool_query, proj, logit_scale
):
    count, length, width = tokens.shape
    rows = count * length
    devices = lax.axis_size("dp")
    experts = devices // SPLIT
    capacity = SPLIT * (3 * rows // (8 * experts) + 1)
    cap = -(-capacity // 16) * 16
    ff = w_in.shape[2]
    me = lax.axis_index("dp").astype(jnp.int32)
    mine = me.reshape(1)

    def swap(values, bits):
        return lax.ppermute(values, "dp", [(i, i ^ bits) for i in range(devices)])

    weights = [w_in[0], w_out[0]]
    weights = weights + [swap(after(w, mine), 1) for w in weights]
    *chunks, place = call(
        functools.partial(dispatch_kernel, experts, cap),
        "dispatch",
        [((cap, width), BF16)] * experts + [((1, rows), jnp.int32)],
        [SMEM] + [VMEM] * 2,
        8,
        flops=FIRST,
    )(mine, route.reshape(1, rows), tokens.reshape(rows, width))
    def expert(own, values, terms, *others):
        outs = [((cap // (n + 1), width), BF16) for n in range(terms)]
        if own:
            outs = [((cap, width), F32), ((cap, 1), F32)]
        return call(
            functools.partial(ffn_kernel, own),
            "own" if own else "other",
            outs,
            [SMEM] + [VMEM] * 7,
            18,
            [pltpu.VMEM((cap, width), BF16), pltpu.VMEM((2, cap, ff), BF16)],
        )(mine, after(values, *others), moe_gain.reshape(1, width), router.T, *weights)

    def finish(k, *others):
        kept, gate = owns[k]
        (final[k],) = call(finish_kernel, "finish", [((cap, width), BF16)], [VMEM] * 4, 4)(
            held[k], gate, after(kept, *others), swap(lefts[k][0], 2)
        )

    held, owns, lefts, final = {0: chunks[0]}, {}, {}, {}
    for k in (1, 2):
        held[k] = swap(chunks[k], SPLIT * k)
    partner = {0: swap(held[0], 2)}
    owns[0] = expert(True, held[0], 0)
    partner[1] = swap(after(held[1], owns[0][0]), 2)
    owns[1] = expert(True, held[1], 0, partner[1], held[2], partner[0])
    partner[2] = swap(after(held[2], owns[0][0]), 2)
    lefts[1] = expert(False, partner[1], 1, owns[1][0])
    owns[2] = expert(True, held[2], 0, lefts[1][0])
    lefts[2] = expert(False, partner[2], 1, owns[2][0])
    finish(1, lefts[2][0])
    last = final[1]
    for k in range(3, experts):
        held[k] = swap(after(chunks[k], held[k - 1]), SPLIT * k)
        partner[k] = swap(after(held[k], lefts[2][0]), 2)
        owns[k] = expert(True, held[k], 0, last)
        last = owns[k][0]
    finish(2, last)
    last = final[2]
    for k in range(3, experts):
        lefts[k] = expert(False, partner[k], 1, last)
        last = lefts[k][0]
    lefts[0] = expert(False, partner[0], 2, last)
    early = [1, 2]
    partial, query = call(
        functools.partial(partial_kernel, early),
        "partial",
        [((rows, width), F32), ((2, width), F32)],
        [VMEM] * 4,
        8,
        [pltpu.VMEM((2 * cap, width), BF16)],
    )(pool_query, place, *[swap(final[k], SPLIT * k) for k in early])
    for k in range(3, experts):
        finish(k, partial)
    kept, gate = owns[0]
    got = [swap(after(term, partial), 2) for term in lefts[0]]
    late = list(range(3, experts))
    mixed, pooled = call(
        functools.partial(combine_kernel, late),
        "combine",
        [((rows, width), BF16), ((4, width), BF16)],
        [SMEM] + [VMEM] * (9 + len(late)),
        20,
        [pltpu.VMEM(((1 + len(late)) * cap, width), BF16)],
    )(
        labels,
        partial,
        held[0],
        gate,
        kept,
        *got,
        place,
        out_gain.reshape(1, width),
        query,
        *[swap(final[k], SPLIT * k) for k in late],
    )
    pieces, bits = [pooled], 1
    while bits < devices:
        pieces.append(swap(jnp.concatenate(pieces, axis=0), bits))
        bits = bits * 2
    d_pooled, loss, grad_proj = call(
        functools.partial(tail_kernel, devices),
        "contrast",
        [((2, width), F32), ((1, 1), F32), ((width, width), F32)],
        [SMEM] * 2 + [VMEM] * (1 + len(pieces)),
        24,
        [pltpu.VMEM((width, width), F32), pltpu.SemaphoreType.DMA((-(-width // TILE),))],
        in_hbm=1,
    )(mine, logit_scale, proj, *pieces)
    return (
        mixed.reshape(count, length, width),
        d_pooled.reshape(count, 2, width),
        grad_proj,
        loss.reshape(1),
    )


def solution(mesh):
    placed = (
        P(("groups", "dp"), None, None),
        P(("groups", "dp"), None, None),
        P(("groups", "dp")),
        P(),
        P(),
        P("dp", None, None),
        P("dp", None, None),
        P(),
        P(),
        P(),
        P(),
    )
    return jax.shard_map(
        on_device,
        mesh=mesh,
        in_specs=placed,
        out_specs=(
            P(("groups", "dp"), None, None),
            P(("groups", "dp"), None, None),
            P("groups", None),
            P("groups"),
        ),
        check_vma=False,
    )
```

```python
import functools
import math

import jax
import jax.numpy as jnp
from jax import lax
from jax.experimental import pallas as pl
from jax.experimental.pallas import tpu as pltpu
from jax.sharding import PartitionSpec as P

HEADS = 16
IMG_TOK = 256
SPLIT = 4
HEAD_DIM = 80
TILE = 256
F32 = jnp.float32
BF16 = jnp.bfloat16
VMEM = pl.BlockSpec(memory_space=pltpu.VMEM)
SMEM = pl.BlockSpec(memory_space=pltpu.SMEM)
ANY = pl.BlockSpec(memory_space=pl.ANY)
FIRST = 20_000_000_000


def iota(shape, dim):
    return lax.broadcasted_iota(jnp.int32, shape, dim)


def dot(a, b, contract=((1,), (0,)), precision=None):
    return lax.dot_general(
        a, b, (contract, ((), ())), precision=precision, preferred_element_type=F32
    )


def split3(values):
    high = values.astype(BF16)
    rest = values - high.astype(F32)
    middle = rest.astype(BF16)
    low = (rest - middle.astype(F32)).astype(BF16)
    return high, middle, low


def layer_norm(values, gain):
    mean = jnp.mean(values, axis=-1, keepdims=True)
    centered = values - mean
    var = jnp.mean(centered * centered, axis=-1, keepdims=True)
    return centered * lax.rsqrt(var + 1e-06) * gain


def dispatch_kernel(experts, cap, mine_ref, ids_ref, tokens_ref, *outs):
    chunks, place_ref = outs[:experts], outs[experts]
    rows = tokens_ref.shape[0]
    ids = ids_ref[...]
    onehot = (iota((experts, rows), 0) == ids).astype(F32)
    earlier = (iota((rows, rows), 0) <= iota((rows, rows), 1)).astype(F32).astype(BF16)
    count = dot(onehot.astype(BF16), earlier)
    slot = jnp.sum((count - 1.0) * onehot, axis=0, keepdims=True).astype(jnp.int32)
    place = (ids ^ (mine_ref[0] // SPLIT)) * cap + slot
    place_ref[...] = place
    select = (iota((experts * cap, rows), 0) == place).astype(F32).astype(BF16)
    buffer = dot(select, tokens_ref[...]).astype(BF16)
    for k in range(experts):
        chunks[k][...] = buffer[k * cap : (k + 1) * cap]


def ffn_kernel(own, mine_ref, rows_ref, gain_ref, router_ref, in_a, out_a, in_b, out_b, *outs):
    *outs, x_ref, hidden_ref = outs
    normed = layer_norm(rows_ref[...].astype(F32), gain_ref[...]).astype(BF16)
    x_ref[...] = normed
    ff, width = out_a.shape
    for index, w_in in enumerate((in_a, in_b)):
        for at in range(0, ff, TILE):
            pre = dot(x_ref[...], w_in[:, at : at + TILE])
            hidden_ref[index, :, at : at + TILE] = jax.nn.gelu(pre, approximate=True).astype(BF16)
    if own:
        router = router_ref[...].astype(F32)
        column = jnp.where(iota(router.shape, 0) == mine_ref[0] // SPLIT, router, 0.0)
        column = jnp.sum(column, axis=0, keepdims=True)
        gate = jnp.sum(normed.astype(F32) * column, axis=1, keepdims=True)
        outs[1][...] = jax.nn.sigmoid(gate)
    for at in range(0, width, TILE):
        total = None
        for index, w_out in enumerate((out_a, out_b)):
            part = dot(hidden_ref[index], w_out[:, at : at + TILE]).astype(BF16).astype(F32)
            total = part if total is None else total + part
        if own:
            outs[0][:, at : at + TILE] = total
        else:
            for out_ref, term in zip(outs, split3(total)):
                out_ref[:, at : at + TILE] = term[: out_ref.shape[0]]


def finish_kernel(tokens_ref, gate_ref, kept_ref, *refs):
    got_ref, *low_refs, mixed_ref = refs
    total = kept_ref[...] + got_ref[...].astype(F32)
    for low_ref in low_refs:
        many = low_ref.shape[0]
        total = jnp.concatenate([total[:many] + low_ref[...].astype(F32), total[many:]], axis=0)
    mixed_ref[...] = (tokens_ref[...].astype(F32) + gate_ref[...] * total).astype(BF16)


def chosen(place, first, many):
    return (iota((many, place.shape[1]), 0) + first == place).astype(F32).astype(BF16)


def heads_of(shape):
    head, feature = iota(shape, 0), iota(shape, 1)
    return (feature >= head * HEAD_DIM) & (feature < (head + 1) * HEAD_DIM)


def partial_kernel(early, query_ref, place_ref, *refs):
    parts, sum_ref, rows_ref, buffer = refs[:-3], *refs[-3:]
    cap, width = parts[0].shape
    for at, part_ref in enumerate(parts):
        buffer[at * cap : (at + 1) * cap] = part_ref[...]
    place = place_ref[...]
    select = jnp.concatenate([chosen(place, k * cap, cap) for k in early], axis=0)
    sum_ref[...] = dot(select, buffer[...], ((0,), (0,)))
    feature = iota((1, width), 1)
    inner = feature - HEAD_DIM * sum(
        (feature >= h * HEAD_DIM).astype(jnp.int32) for h in range(1, HEADS)
    )
    spread = (iota((HEAD_DIM, width), 0) == inner).astype(F32).astype(BF16)
    for modal in range(2):
        wide = sum(dot(term, spread) for term in split3(query_ref[modal]))
        wide = jnp.where(heads_of((HEADS, width)), wide, 0.0)
        rows_ref[modal : modal + 1] = jnp.sum(wide, axis=0, keepdims=True)


def combine_kernel(late, *refs):
    label_ref, sum_ref, tokens_ref, gate_ref, kept_ref, high_ref, low_ref, place_ref = refs[:8]
    gain_ref, query_ref, *backs, mixed_ref, pooled_ref, buffer = refs[8:]
    cap = kept_ref.shape[0]
    rows, width = mixed_ref.shape
    finish_kernel(tokens_ref, gate_ref, kept_ref, high_ref, low_ref, buffer.at[:cap])
    for at, back_ref in enumerate(backs):
        buffer[(at + 1) * cap : (at + 2) * cap] = back_ref[...]
    place = place_ref[...]
    select = jnp.concatenate([chosen(place, k * cap, cap) for k in [0] + late], axis=0)
    mixed = sum_ref[...] + dot(select, buffer[...], ((0,), (0,)))
    mixed_ref[...] = mixed.astype(BF16)
    z = layer_norm(mixed, gain_ref[...])
    head, feature = iota((width, HEADS), 1), iota((width, HEADS), 0)
    member = (feature >= head * HEAD_DIM) & (feature < (head + 1) * HEAD_DIM)
    member = member.astype(F32).astype(BF16)
    spread = heads_of((HEADS, width)).astype(F32).astype(BF16)
    for modal, (lower, upper) in enumerate(((0, IMG_TOK), (IMG_TOK, rows))):
        piece = z[lower:upper]
        scores = sum(dot(term, member) for term in split3(piece * query_ref[modal : modal + 1]))
        scores = scores / math.sqrt(HEAD_DIM)
        weights = jnp.exp(scores - jnp.max(scores, axis=0, keepdims=True))
        weights = weights / jnp.sum(weights, axis=0, keepdims=True)
        wide = sum(dot(term, spread) for term in split3(weights))
        pooled_ref[modal : modal + 1] = jnp.sum(wide * piece, axis=0, keepdims=True).astype(BF16)
    pooled_ref[2:4] = jnp.full((2, width), label_ref[0], jnp.int32).astype(F32).astype(BF16)


def tail_kernel(
    pairs, mine_ref, scale_ref, proj_ref, *refs
):
    pieces, (d_pooled_ref, loss_ref, grad_ref, store, sems) = refs[:-5], refs[-5:]
    exact = lax.Precision.HIGHEST
    me, scale = mine_ref[0], scale_ref[0]
    levels = len(pieces) - 1

    def held_at(pair):
        apart = pair ^ me
        return sum(((apart >> level) & 1) << (levels - 1 - level) for level in range(levels)) * 4

    at, pooled, labels = 0, 0.0, 0.0
    for piece in pieces:
        many = piece.shape[0]
        row, col = iota((2 * pairs, many), 0), iota((2 * pairs, many), 1) + at
        wanted = jnp.where(row < pairs, held_at(row), held_at(row - pairs) + 1)
        pooled = pooled + dot((col == wanted).astype(F32).astype(BF16), piece[...])
        row, col = iota((pairs, many), 0), iota((pairs, many), 1) + at
        wanted = (col == held_at(row) + 2).astype(F32).astype(BF16)
        labels = labels + dot(wanted, piece[:, :128])
        at = at + many
    pooled, labels = pooled.astype(BF16), labels[:, :1]
    emb = dot(pooled, proj_ref[...])
    norm = jnp.sqrt(jnp.sum(emb * emb, axis=-1, keepdims=True) + 1e-06)
    unit = emb / norm
    image, text = unit[:pairs], unit[pairs:]
    logits = scale * dot(image, text, ((1,), (1,)), exact)
    target = (labels == iota((pairs, pairs), 1).astype(F32)).astype(F32)
    row_top = jnp.max(logits, axis=1, keepdims=True)
    row_exp = jnp.exp(logits - row_top)
    row_total = jnp.sum(row_exp, axis=1, keepdims=True)
    row_lse = jnp.log(row_total) + row_top
    col_top = jnp.max(logits, axis=0, keepdims=True)
    col_exp = jnp.exp(logits - col_top)
    col_total = jnp.sum(col_exp, axis=0, keepdims=True)
    col_lse = jnp.log(col_total) + col_top
    matched = jnp.sum(jnp.sum(logits * target, axis=1, keepdims=True), axis=0, keepdims=True)
    total = jnp.sum(row_lse, axis=0, keepdims=True) + jnp.sum(col_lse, axis=1, keepdims=True)
    loss_ref[...] = (total - 2.0 * matched) / (2.0 * pairs)
    grad = scale * (row_exp / row_total + col_exp / col_total - 2.0 * target) / (2.0 * pairs)
    d_image = dot(grad, text, precision=exact)
    d_text = dot(grad, image, ((0,), (0,)), exact)
    d_unit = jnp.concatenate([d_image, d_text], axis=0)
    d_emb = (d_unit - unit * jnp.sum(unit * d_unit, axis=-1, keepdims=True)) / norm
    terms = jnp.concatenate(split3(d_emb), axis=0)
    thrice = jnp.concatenate([pooled] * 3, axis=0)
    copies = []
    for at in range(0, pooled.shape[1], TILE):
        store[at : at + TILE] = dot(thrice[:, at : at + TILE], terms, ((0,), (0,)))
        copies.append(
            pltpu.make_async_copy(
                store.at[at : at + TILE], grad_ref.at[at : at + TILE], sems.at[at // TILE]
            )
        )
        copies[-1].start()
    row = iota(d_emb.shape, 0)
    own = [
        jnp.sum(jnp.where(row == me + modal * pairs, d_emb, 0.0), axis=0, keepdims=True)
        for modal in range(2)
    ]
    terms = jnp.concatenate(split3(jnp.concatenate(own, axis=0)), axis=0)
    back = dot(terms, proj_ref[...], ((1,), (1,)))
    d_pooled_ref[...] = back[0:2] + back[2:4] + back[4:6]
    for copy in copies:
        copy.wait()


def call(kernel, name, outs, specs, limit, scratch=(), flops=0, in_hbm=0):
    return pl.pallas_call(
        kernel,
        out_shape=[jax.ShapeDtypeStruct(*o) for o in outs],
        in_specs=specs,
        out_specs=[VMEM] * (len(outs) - in_hbm) + [ANY] * in_hbm,
        scratch_shapes=list(scratch),
        compiler_params=pltpu.CompilerParams(vmem_limit_bytes=limit * 1024 * 1024),
        cost_estimate=pl.CostEstimate(flops=flops, bytes_accessed=0, transcendentals=0),
        name=name,
    )


def after(values, *others):
    return lax.optimization_barrier((values,) + others)[0] if others else values


def on_device(
    tokens, route, labels, moe_gain, router, w_in, w_out, out_gain, pool_query, proj, logit_scale
):
    count, length, width = tokens.shape
    rows = count * length
    devices = lax.axis_size("dp")
    experts = devices // SPLIT
    capacity = SPLIT * (3 * rows // (8 * experts) + 1)
    cap = -(-capacity // 16) * 16
    ff = w_in.shape[2]
    me = lax.axis_index("dp").astype(jnp.int32)
    mine = me.reshape(1)

    def swap(values, bits):
        return lax.ppermute(values, "dp", [(i, i ^ bits) for i in range(devices)])

    weights = [w_in[0], w_out[0]]
    weights = weights + [swap(after(w, mine), 1) for w in weights]
    *chunks, place = call(
        functools.partial(dispatch_kernel, experts, cap),
        "dispatch",
        [((cap, width), BF16)] * experts + [((1, rows), jnp.int32)],
        [SMEM] + [VMEM] * 2,
        8,
        flops=FIRST,
    )(mine, route.reshape(1, rows), tokens.reshape(rows, width))
    def expert(own, values, terms, *others):
        outs = [((cap // (n + 1), width), BF16) for n in range(terms)]
        if own:
            outs = [((cap, width), F32), ((cap, 1), F32)]
        return call(
            functools.partial(ffn_kernel, own),
            "own" if own else "other",
            outs,
            [SMEM] + [VMEM] * 7,
            18,
            [pltpu.VMEM((cap, width), BF16), pltpu.VMEM((2, cap, ff), BF16)],
        )(mine, after(values, *others), moe_gain.reshape(1, width), router.T, *weights)

    def finish(k, *others):
        kept, gate = owns[k]
        (final[k],) = call(finish_kernel, "finish", [((cap, width), BF16)], [VMEM] * 4, 4)(
            held[k], gate, after(kept, *others), swap(lefts[k][0], 2)
        )

    held, owns, lefts, final = {0: chunks[0]}, {}, {}, {}
    for k in (1, 2):
        held[k] = swap(chunks[k], SPLIT * k)
    partner = {0: swap(held[0], 2)}
    owns[0] = expert(True, held[0], 0)
    partner[1] = swap(after(held[1], owns[0][0]), 2)
    owns[2] = expert(True, held[2], 0, held[1], partner[0])
    owns[1] = expert(True, held[1], 0, partner[1], owns[2][0])
    partner[2] = swap(after(held[2], owns[0][0]), 2)
    lefts[1] = expert(False, partner[1], 1, owns[1][0])
    lefts[2] = expert(False, partner[2], 1, lefts[1][0])
    finish(1, lefts[2][0])
    last = final[1]
    for k in range(3, experts):
        held[k] = swap(after(chunks[k], held[k - 1]), SPLIT * k)
        partner[k] = swap(after(held[k], lefts[2][0]), 2)
        owns[k] = expert(True, held[k], 0, last)
        last = owns[k][0]
    finish(2, last)
    last = final[2]
    for k in range(3, experts):
        lefts[k] = expert(False, partner[k], 1, last)
        last = lefts[k][0]
    lefts[0] = expert(False, partner[0], 2, last)
    early = [1, 2]
    partial, query = call(
        functools.partial(partial_kernel, early),
        "partial",
        [((rows, width), F32), ((2, width), F32)],
        [VMEM] * 4,
        8,
        [pltpu.VMEM((2 * cap, width), BF16)],
    )(pool_query, place, *[swap(final[k], SPLIT * k) for k in early])
    for k in range(3, experts):
        finish(k, partial)
    kept, gate = owns[0]
    got = [swap(after(term, partial), 2) for term in lefts[0]]
    late = list(range(3, experts))
    mixed, pooled = call(
        functools.partial(combine_kernel, late),
        "combine",
        [((rows, width), BF16), ((4, width), BF16)],
        [SMEM] + [VMEM] * (9 + len(late)),
        20,
        [pltpu.VMEM(((1 + len(late)) * cap, width), BF16)],
    )(
        labels,
        partial,
        held[0],
        gate,
        kept,
        *got,
        place,
        out_gain.reshape(1, width),
        query,
        *[swap(final[k], SPLIT * k) for k in late],
    )
    pieces, bits = [pooled], devices // 2
    while bits:
        pieces.append(swap(jnp.concatenate(pieces, axis=0), bits))
        bits = bits // 2
    d_pooled, loss, grad_proj = call(
        functools.partial(tail_kernel, devices),
        "contrast",
        [((2, width), F32), ((1, 1), F32), ((width, width), F32)],
        [SMEM] * 2 + [VMEM] * (1 + len(pieces)),
        24,
        [pltpu.VMEM((width, width), F32), pltpu.SemaphoreType.DMA((-(-width // TILE),))],
        in_hbm=1,
    )(mine, logit_scale, proj, *pieces)
    return (
        mixed.reshape(count, length, width),
        d_pooled.reshape(count, 2, width),
        grad_proj,
        loss.reshape(1),
    )


def solution(mesh):
    placed = (
        P(("groups", "dp"), None, None),
        P(("groups", "dp"), None, None),
        P(("groups", "dp")),
        P(),
        P(),
        P("dp", None, None),
        P("dp", None, None),
        P(),
        P(),
        P(),
        P(),
    )
    return jax.shard_map(
        on_device,
        mesh=mesh,
        in_specs=placed,
        out_specs=(
            P(("groups", "dp"), None, None),
            P(("groups", "dp"), None, None),
            P("groups", None),
            P("groups"),
        ),
        check_vma=False,
    )
```

```python
import functools
import math

import jax
import jax.numpy as jnp
from jax import lax
from jax.experimental import pallas as pl
from jax.experimental.pallas import tpu as pltpu
from jax.sharding import PartitionSpec as P

HEADS = 16
IMG_TOK = 256
SPLIT = 4
HEAD_DIM = 80
TILE = 256
F32 = jnp.float32
BF16 = jnp.bfloat16
VMEM = pl.BlockSpec(memory_space=pltpu.VMEM)
SMEM = pl.BlockSpec(memory_space=pltpu.SMEM)
ANY = pl.BlockSpec(memory_space=pl.ANY)
FIRST = 20_000_000_000


def iota(shape, dim):
    return lax.broadcasted_iota(jnp.int32, shape, dim)


def dot(a, b, contract=((1,), (0,)), precision=None):
    return lax.dot_general(
        a, b, (contract, ((), ())), precision=precision, preferred_element_type=F32
    )


def split3(values):
    high = values.astype(BF16)
    rest = values - high.astype(F32)
    middle = rest.astype(BF16)
    low = (rest - middle.astype(F32)).astype(BF16)
    return high, middle, low


def layer_norm(values, gain):
    mean = jnp.mean(values, axis=-1, keepdims=True)
    centered = values - mean
    var = jnp.mean(centered * centered, axis=-1, keepdims=True)
    return centered * lax.rsqrt(var + 1e-06) * gain


def dispatch_kernel(experts, cap, mine_ref, ids_ref, tokens_ref, *outs):
    chunks, place_ref = outs[:experts], outs[experts]
    rows = tokens_ref.shape[0]
    ids = ids_ref[...]
    onehot = (iota((experts, rows), 0) == ids).astype(F32)
    earlier = (iota((rows, rows), 0) <= iota((rows, rows), 1)).astype(F32).astype(BF16)
    count = dot(onehot.astype(BF16), earlier)
    slot = jnp.sum((count - 1.0) * onehot, axis=0, keepdims=True).astype(jnp.int32)
    place = (ids ^ (mine_ref[0] // SPLIT)) * cap + slot
    place_ref[...] = place
    select = (iota((experts * cap, rows), 0) == place).astype(F32).astype(BF16)
    buffer = dot(select, tokens_ref[...]).astype(BF16)
    for k in range(experts):
        chunks[k][...] = buffer[k * cap : (k + 1) * cap]


def ffn_kernel(own, mine_ref, rows_ref, gain_ref, router_ref, in_a, out_a, in_b, out_b, *outs):
    *outs, x_ref, hidden_ref = outs
    normed = layer_norm(rows_ref[...].astype(F32), gain_ref[...]).astype(BF16)
    x_ref[...] = normed
    ff, width = out_a.shape
    for index, w_in in enumerate((in_a, in_b)):
        for at in range(0, ff, TILE):
            pre = dot(x_ref[...], w_in[:, at : at + TILE])
            hidden_ref[index, :, at : at + TILE] = jax.nn.gelu(pre, approximate=True).astype(BF16)
    if own:
        router = router_ref[...].astype(F32)
        column = jnp.where(iota(router.shape, 0) == mine_ref[0] // SPLIT, router, 0.0)
        column = jnp.sum(column, axis=0, keepdims=True)
        gate = jnp.sum(normed.astype(F32) * column, axis=1, keepdims=True)
        outs[1][...] = jax.nn.sigmoid(gate)
    for at in range(0, width, TILE):
        total = None
        for index, w_out in enumerate((out_a, out_b)):
            part = dot(hidden_ref[index], w_out[:, at : at + TILE]).astype(BF16).astype(F32)
            total = part if total is None else total + part
        if own:
            outs[0][:, at : at + TILE] = total
        else:
            for out_ref, term in zip(outs, split3(total)):
                out_ref[:, at : at + TILE] = term[: out_ref.shape[0]]


def finish_kernel(tokens_ref, gate_ref, kept_ref, *refs):
    got_ref, *low_refs, mixed_ref = refs
    total = kept_ref[...] + got_ref[...].astype(F32)
    for low_ref in low_refs:
        many = low_ref.shape[0]
        total = jnp.concatenate([total[:many] + low_ref[...].astype(F32), total[many:]], axis=0)
    mixed_ref[...] = (tokens_ref[...].astype(F32) + gate_ref[...] * total).astype(BF16)


def chosen(place, first, many):
    return (iota((many, place.shape[1]), 0) + first == place).astype(F32).astype(BF16)


def heads_of(shape):
    head, feature = iota(shape, 0), iota(shape, 1)
    return (feature >= head * HEAD_DIM) & (feature < (head + 1) * HEAD_DIM)


def partial_kernel(early, late, query_ref, place_ref, *refs):
    parts, (sum_ref, rows_ref, select_ref, buffer) = refs[:-4], refs[-4:]
    cap, width = parts[0].shape
    for at, part_ref in enumerate(parts):
        buffer[at * cap : (at + 1) * cap] = part_ref[...]
    place = place_ref[...]
    select = jnp.concatenate([chosen(place, k * cap, cap) for k in early], axis=0)
    sum_ref[...] = dot(select, buffer[...], ((0,), (0,)))
    select = jnp.concatenate([chosen(place, k * cap, cap) for k in [0] + late], axis=0)
    select_ref[...] = select.T
    feature = iota((1, width), 1)
    inner = feature - HEAD_DIM * sum(
        (feature >= h * HEAD_DIM).astype(jnp.int32) for h in range(1, HEADS)
    )
    spread = (iota((HEAD_DIM, width), 0) == inner).astype(F32).astype(BF16)
    for modal in range(2):
        wide = sum(dot(term, spread) for term in split3(query_ref[modal]))
        wide = jnp.where(heads_of((HEADS, width)), wide, 0.0)
        rows_ref[modal : modal + 1] = jnp.sum(wide, axis=0, keepdims=True)


def combine_kernel(*refs):
    label_ref, sum_ref, tokens_ref, gate_ref, kept_ref, high_ref, low_ref, select_ref = refs[:8]
    gain_ref, query_ref, *backs, mixed_ref, pooled_ref, buffer = refs[8:]
    cap = kept_ref.shape[0]
    rows, width = mixed_ref.shape
    finish_kernel(tokens_ref, gate_ref, kept_ref, high_ref, low_ref, buffer.at[:cap])
    for at, back_ref in enumerate(backs):
        buffer[(at + 1) * cap : (at + 2) * cap] = back_ref[...]
    mixed = sum_ref[...] + dot(select_ref[...], buffer[...])
    mixed_ref[...] = mixed.astype(BF16)
    z = layer_norm(mixed, gain_ref[...])
    head, feature = iota((width, HEADS), 1), iota((width, HEADS), 0)
    member = (feature >= head * HEAD_DIM) & (feature < (head + 1) * HEAD_DIM)
    member = member.astype(F32).astype(BF16)
    spread = heads_of((HEADS, width)).astype(F32).astype(BF16)
    for modal, (lower, upper) in enumerate(((0, IMG_TOK), (IMG_TOK, rows))):
        piece = z[lower:upper]
        scores = sum(dot(term, member) for term in split3(piece * query_ref[modal : modal + 1]))
        scores = scores / math.sqrt(HEAD_DIM)
        weights = jnp.exp(scores - jnp.max(scores, axis=0, keepdims=True))
        weights = weights / jnp.sum(weights, axis=0, keepdims=True)
        wide = sum(dot(term, spread) for term in split3(weights))
        pooled_ref[modal : modal + 1] = jnp.sum(wide * piece, axis=0, keepdims=True).astype(BF16)
    pooled_ref[2:4] = jnp.full((2, width), label_ref[0], jnp.int32).astype(F32).astype(BF16)


def tail_kernel(
    pairs, mine_ref, scale_ref, proj_ref, *refs
):
    pieces, (d_pooled_ref, loss_ref, grad_ref, store, sems) = refs[:-5], refs[-5:]
    exact = lax.Precision.HIGHEST
    me, scale = mine_ref[0], scale_ref[0]
    levels = len(pieces) - 1

    def held_at(pair):
        apart = pair ^ me
        return sum(((apart >> level) & 1) << (levels - 1 - level) for level in range(levels)) * 4

    at, pooled, labels = 0, 0.0, 0.0
    for piece in pieces:
        many = piece.shape[0]
        row, col = iota((2 * pairs, many), 0), iota((2 * pairs, many), 1) + at
        wanted = jnp.where(row < pairs, held_at(row), held_at(row - pairs) + 1)
        pooled = pooled + dot((col == wanted).astype(F32).astype(BF16), piece[...])
        row, col = iota((pairs, many), 0), iota((pairs, many), 1) + at
        wanted = (col == held_at(row) + 2).astype(F32).astype(BF16)
        labels = labels + dot(wanted, piece[:, :128])
        at = at + many
    pooled, labels = pooled.astype(BF16), labels[:, :1]
    emb = dot(pooled, proj_ref[...])
    norm = jnp.sqrt(jnp.sum(emb * emb, axis=-1, keepdims=True) + 1e-06)
    unit = emb / norm
    image, text = unit[:pairs], unit[pairs:]
    logits = scale * dot(image, text, ((1,), (1,)), exact)
    target = (labels == iota((pairs, pairs), 1).astype(F32)).astype(F32)
    row_top = jnp.max(logits, axis=1, keepdims=True)
    row_exp = jnp.exp(logits - row_top)
    row_total = jnp.sum(row_exp, axis=1, keepdims=True)
    row_lse = jnp.log(row_total) + row_top
    col_top = jnp.max(logits, axis=0, keepdims=True)
    col_exp = jnp.exp(logits - col_top)
    col_total = jnp.sum(col_exp, axis=0, keepdims=True)
    col_lse = jnp.log(col_total) + col_top
    matched = jnp.sum(jnp.sum(logits * target, axis=1, keepdims=True), axis=0, keepdims=True)
    total = jnp.sum(row_lse, axis=0, keepdims=True) + jnp.sum(col_lse, axis=1, keepdims=True)
    loss_ref[...] = (total - 2.0 * matched) / (2.0 * pairs)
    grad = scale * (row_exp / row_total + col_exp / col_total - 2.0 * target) / (2.0 * pairs)
    d_image = dot(grad, text, precision=exact)
    d_text = dot(grad, image, ((0,), (0,)), exact)
    d_unit = jnp.concatenate([d_image, d_text], axis=0)
    d_emb = (d_unit - unit * jnp.sum(unit * d_unit, axis=-1, keepdims=True)) / norm
    terms = jnp.concatenate(split3(d_emb), axis=0)
    thrice = jnp.concatenate([pooled] * 3, axis=0)
    copies = []
    for at in range(0, pooled.shape[1], TILE):
        store[at : at + TILE] = dot(thrice[:, at : at + TILE], terms, ((0,), (0,)))
        copies.append(
            pltpu.make_async_copy(
                store.at[at : at + TILE], grad_ref.at[at : at + TILE], sems.at[at // TILE]
            )
        )
        copies[-1].start()
    row = iota(d_emb.shape, 0)
    own = [
        jnp.sum(jnp.where(row == me + modal * pairs, d_emb, 0.0), axis=0, keepdims=True)
        for modal in range(2)
    ]
    terms = jnp.concatenate(split3(jnp.concatenate(own, axis=0)), axis=0)
    back = dot(terms, proj_ref[...], ((1,), (1,)))
    d_pooled_ref[...] = back[0:2] + back[2:4] + back[4:6]
    for copy in copies:
        copy.wait()


def call(kernel, name, outs, specs, limit, scratch=(), flops=0, in_hbm=0):
    return pl.pallas_call(
        kernel,
        out_shape=[jax.ShapeDtypeStruct(*o) for o in outs],
        in_specs=specs,
        out_specs=[VMEM] * (len(outs) - in_hbm) + [ANY] * in_hbm,
        scratch_shapes=list(scratch),
        compiler_params=pltpu.CompilerParams(vmem_limit_bytes=limit * 1024 * 1024),
        cost_estimate=pl.CostEstimate(flops=flops, bytes_accessed=0, transcendentals=0),
        name=name,
    )


def after(values, *others):
    return lax.optimization_barrier((values,) + others)[0] if others else values


def on_device(
    tokens, route, labels, moe_gain, router, w_in, w_out, out_gain, pool_query, proj, logit_scale
):
    count, length, width = tokens.shape
    rows = count * length
    devices = lax.axis_size("dp")
    experts = devices // SPLIT
    capacity = SPLIT * (3 * rows // (8 * experts) + 1)
    cap = -(-capacity // 16) * 16
    ff = w_in.shape[2]
    me = lax.axis_index("dp").astype(jnp.int32)
    mine = me.reshape(1)

    def swap(values, bits):
        return lax.ppermute(values, "dp", [(i, i ^ bits) for i in range(devices)])

    weights = [w_in[0], w_out[0]]
    weights = weights + [swap(after(w, mine), 1) for w in weights]
    *chunks, place = call(
        functools.partial(dispatch_kernel, experts, cap),
        "dispatch",
        [((cap, width), BF16)] * experts + [((1, rows), jnp.int32)],
        [SMEM] + [VMEM] * 2,
        8,
        flops=FIRST,
    )(mine, route.reshape(1, rows), tokens.reshape(rows, width))
    def expert(own, values, terms, *others):
        outs = [((cap // (n + 1), width), BF16) for n in range(terms)]
        if own:
            outs = [((cap, width), F32), ((cap, 1), F32)]
        return call(
            functools.partial(ffn_kernel, own),
            "own" if own else "other",
            outs,
            [SMEM] + [VMEM] * 7,
            18,
            [pltpu.VMEM((cap, width), BF16), pltpu.VMEM((2, cap, ff), BF16)],
        )(mine, after(values, *others), moe_gain.reshape(1, width), router.T, *weights)

    def finish(k, *others):
        kept, gate = owns[k]
        (final[k],) = call(finish_kernel, "finish", [((cap, width), BF16)], [VMEM] * 4, 4)(
            held[k], gate, after(kept, *others), swap(lefts[k][0], 2)
        )

    held, owns, lefts, final = {0: chunks[0]}, {}, {}, {}
    for k in (1, 2):
        held[k] = swap(chunks[k], SPLIT * k)
    partner = {0: swap(held[0], 2)}
    owns[0] = expert(True, held[0], 0)
    partner[1] = swap(after(held[1], owns[0][0]), 2)
    owns[2] = expert(True, held[2], 0, held[1], partner[0])
    owns[1] = expert(True, held[1], 0, partner[1], owns[2][0])
    partner[2] = swap(after(held[2], owns[0][0]), 2)
    lefts[1] = expert(False, partner[1], 1, owns[1][0])
    lefts[2] = expert(False, partner[2], 1, lefts[1][0])
    finish(1, lefts[2][0])
    last = final[1]
    for k in range(3, experts):
        held[k] = swap(after(chunks[k], held[k - 1]), SPLIT * k)
        partner[k] = swap(after(held[k], lefts[2][0]), 2)
        owns[k] = expert(True, held[k], 0, last)
        last = owns[k][0]
    finish(2, last)
    last = final[2]
    for k in range(3, experts):
        lefts[k] = expert(False, partner[k], 1, last)
        last = lefts[k][0]
    lefts[0] = expert(False, partner[0], 2, last)
    early = [1, 2]
    late = list(range(3, experts))
    partial, query, select = call(
        functools.partial(partial_kernel, early, late),
        "partial",
        [((rows, width), F32), ((2, width), F32), ((rows, (1 + len(late)) * cap), BF16)],
        [VMEM] * 4,
        8,
        [pltpu.VMEM((2 * cap, width), BF16)],
    )(pool_query, place, *[swap(final[k], SPLIT * k) for k in early])
    for k in range(3, experts):
        finish(k, partial)
    kept, gate = owns[0]
    got = [swap(after(term, partial), 2) for term in lefts[0]]
    mixed, pooled = call(
        combine_kernel,
        "combine",
        [((rows, width), BF16), ((4, width), BF16)],
        [SMEM] + [VMEM] * (9 + len(late)),
        20,
        [pltpu.VMEM(((1 + len(late)) * cap, width), BF16)],
    )(
        labels,
        partial,
        held[0],
        gate,
        kept,
        *got,
        select,
        out_gain.reshape(1, width),
        query,
        *[swap(final[k], SPLIT * k) for k in late],
    )
    pieces, bits = [pooled], devices // 2
    while bits:
        pieces.append(swap(jnp.concatenate(pieces, axis=0), bits))
        bits = bits // 2
    d_pooled, loss, grad_proj = call(
        functools.partial(tail_kernel, devices),
        "contrast",
        [((2, width), F32), ((1, 1), F32), ((width, width), F32)],
        [SMEM] * 2 + [VMEM] * (1 + len(pieces)),
        24,
        [pltpu.VMEM((width, width), F32), pltpu.SemaphoreType.DMA((-(-width // TILE),))],
        in_hbm=1,
    )(mine, logit_scale, proj, *pieces)
    return (
        mixed.reshape(count, length, width),
        d_pooled.reshape(count, 2, width),
        grad_proj,
        loss.reshape(1),
    )


def solution(mesh):
    placed = (
        P(("groups", "dp"), None, None),
        P(("groups", "dp"), None, None),
        P(("groups", "dp")),
        P(),
        P(),
        P("dp", None, None),
        P("dp", None, None),
        P(),
        P(),
        P(),
        P(),
    )
    return jax.shard_map(
        on_device,
        mesh=mesh,
        in_specs=placed,
        out_specs=(
            P(("groups", "dp"), None, None),
            P(("groups", "dp"), None, None),
            P("groups", None),
            P("groups"),
        ),
        check_vma=False,
    )
```
